32 devices in a mesh: grp: 8 (over z, core), seq: 4 (over y, x).
Axes of the slice: x: 2, y: 2, z: 4, core: 2. Of those that a mesh axis runs over, the one named last changes fastest.
Arguments:
- prompt_len: int32 [8], replicated, may hold values from 128 to 256, as said below
- resp_len: int32 [8, 4], replicated, may hold values from 1 to 128, as said below
- resp_host: int32 [8, 4], replicated, may hold values from 0 to 7, as said below
- q_prompt: bfloat16 [8, 256, 4096], P('grp', 'seq'), may hold values from -5 to 5
- k_prompt: bfloat16 [8, 256, 512], P('grp', 'seq'), may hold values from -5 to 5
- v_prompt: bfloat16 [8, 256, 512], P('grp', 'seq'), may hold values from -6 to 6
- g_prompt: bfloat16 [8, 256, 4096], P('grp', 'seq'), may hold values from -6 to 6
- q_resp: bfloat16 [8, 512, 4096], P('grp', 'seq'), may hold values from -5 to 5
- k_resp: bfloat16 [8, 512, 512], P('grp', 'seq'), may hold values from -5 to 5
- v_resp: bfloat16 [8, 512, 512], P('grp', 'seq'), may hold values from -6 to 6
- g_resp: bfloat16 [8, 512, 4096], P('grp', 'seq'), may hold values from -6 to 6
Outputs:
- out_prompt: bfloat16 [8, 256, 4096], P('grp', 'seq')
- out_resp: bfloat16 [8, 512, 4096], P('grp', 'seq')
- dq_prompt: bfloat16 [8, 256, 4096], P('grp', 'seq')
- dq_resp: bfloat16 [8, 512, 4096], P('grp', 'seq')
- dk_prompt: bfloat16 [8, 256, 512], P('grp', 'seq')
- dv_prompt: bfloat16 [8, 256, 512], P('grp', 'seq')
- dk_resp: bfloat16 [8, 512, 512], P('grp', 'seq')
- dv_resp: bfloat16 [8, 512, 512], P('grp', 'seq')
The draws below stay inside these ranges and needn't reach their ends.
Inputs may be any that keep to these rules, and one draw needn't show every extreme that they name: `prompt_len`: one prompt in every draw has all 256 rows live. `resp_len`: every prompt has a response of 128 rows. `resp_host`: response r of prompt p runs on group 2 * (p // 2) + h // 4 at seq index h % 4, h its entry; every device hosts exactly one response, and in each pair of groups some response of each prompt runs on the other group of the pair.
All inputs are finite; a program needn't handle non-finite values.
Results may differ from the reference program's by a relative error of at most 0.012.
The reference program's roundings to bfloat16 on the way count: a program that leaves them out, or rounds other values in their place, can miss the bound.
Values may be sent and summed in bfloat16 or wider, within the bound.
No kernel may reach another device: no remote copies, remote signals or barrier semaphores. Data moves between devices by JAX's collectives and lax.ppermute only.
A program may use at most 128 MiB of HBM per device.

```python
import jax
import jax.numpy as jnp
from jax import lax

HQ = 32
KVH = 4
DH = 128
R_SLOTS = 128
GROUPS = 8
PROMPT = 256
RESPS = 4
RTOK = 512
N_SEQ = 4


def draw_prompt_len(key, part):
    key = jax.random.fold_in(key, 1)
    first, second = jax.random.split(key)
    lengths = jax.random.randint(first, (GROUPS,), PROMPT // 2, PROMPT + 1)
    fullest = jax.random.randint(second, (), 0, GROUPS)
    return jnp.where(jnp.arange(GROUPS) == fullest, PROMPT, lengths).astype(jnp.int32)


def draw_resp_len(key, part):
    key = jax.random.fold_in(key, 2)
    first, second, third = jax.random.split(key, 3)
    level = jax.random.randint(first, (GROUPS, RESPS), 0, 4)
    widest = jnp.right_shift(jnp.full((GROUPS, RESPS), R_SLOTS, jnp.int32), level.astype(jnp.int32))
    trimmed = jax.random.randint(second, (GROUPS, RESPS), 0, 2 ** 30) % (widest // 2)
    lengths = widest - trimmed
    fullest = jax.random.randint(third, (GROUPS,), 0, RESPS)
    return jnp.where(jnp.arange(RESPS)[None, :] == fullest[:, None], R_SLOTS, lengths).astype(jnp.int32)


def draw_resp_host(key, part):
    key = jax.random.fold_in(key, 3)

    def pair_hosts(pair_key):
        first, second, third = jax.random.split(pair_key, 3)
        ranks_a = jax.random.permutation(first, RESPS)
        ranks_b = jax.random.permutation(second, RESPS)
        crossing = jax.random.randint(third, (), 1, RESPS)
        hosts_a = jnp.where(ranks_a < crossing, RESPS + ranks_a, ranks_a)
        hosts_b = jnp.where(ranks_b < crossing, ranks_b, RESPS + ranks_b)
        return jnp.stack([hosts_a, hosts_b])
    hosts = jax.vmap(pair_hosts)(jax.random.split(key, GROUPS // 2))
    return hosts.reshape(GROUPS, RESPS).astype(jnp.int32)


def draw_q_prompt(key, part):
    key = jax.random.fold_in(key, 11)
    first = jax.random.fold_in(key, 0)
    shape = (GROUPS, PROMPT, HQ * DH)
    field = jnp.clip(jax.random.normal(first, shape), -5.0, 5.0)
    return field.astype(jnp.bfloat16)


def draw_k_prompt(key, part):
    key = jax.random.fold_in(key, 12)
    first = jax.random.fold_in(key, 0)
    shape = (GROUPS, PROMPT, KVH * DH)
    field = jnp.clip(jax.random.normal(first, shape), -5.0, 5.0)
    return field.astype(jnp.bfloat16)


def draw_q_resp(key, part):
    key = jax.random.fold_in(key, 13)
    first = jax.random.fold_in(key, 0)
    shape = (GROUPS, RTOK, HQ * DH)
    field = jnp.clip(jax.random.normal(first, shape), -5.0, 5.0)
    return field.astype(jnp.bfloat16)


def draw_k_resp(key, part):
    key = jax.random.fold_in(key, 14)
    first = jax.random.fold_in(key, 0)
    shape = (GROUPS, RTOK, KVH * DH)
    field = jnp.clip(jax.random.normal(first, shape), -5.0, 5.0)
    return field.astype(jnp.bfloat16)


def block_scale(own_key, dims, pieces, least, top_value):
    def one(dim, parts):
        heights = jax.random.uniform(jax.random.fold_in(jax.random.fold_in(own_key, 6), dim), (parts,), jnp.float32, least / len(pieces), top_value / len(pieces))
        return jnp.repeat(jnp.exp(heights), dims[dim] // parts).reshape((-1,) + (1,) * (len(dims) - dim - 1))

    level = one(*pieces[0])
    for cut in pieces[1:]:
        level = level * one(*cut)
    return level


def noise(rng, extent, deviation, limit, cuts=(), kind=jnp.bfloat16):
    entries = deviation * jax.random.normal(rng, extent, jnp.float32)
    if cuts:
        entries = entries * block_scale(rng, extent, cuts, -0.22, 0.18)
    return jnp.clip(entries, -limit, limit).astype(kind)


def setup_inputs(seed: int = 0) -> dict:
    arg_keys = jax.random.split(jax.random.key(seed), 12)
    return {
        "prompt_len": draw_prompt_len(jax.random.fold_in(arg_keys[11], 71), 0),
        "resp_len": draw_resp_len(jax.random.fold_in(arg_keys[11], 71), 0),
        "resp_host": draw_resp_host(jax.random.fold_in(arg_keys[11], 71), 0),
        "q_prompt": draw_q_prompt(jax.random.fold_in(arg_keys[11], 71), 0),
        "k_prompt": draw_k_prompt(jax.random.fold_in(arg_keys[11], 71), 0),
        "v_prompt": noise(arg_keys[5], (GROUPS, PROMPT, KVH * DH), 1.0, 6.0, ((0, 8), (1, 4))),
        "g_prompt": noise(arg_keys[6], (GROUPS, PROMPT, HQ * DH), 1.0, 6.0, ((0, 8), (1, 4))),
        "q_resp": draw_q_resp(jax.random.fold_in(arg_keys[11], 71), 0),
        "k_resp": draw_k_resp(jax.random.fold_in(arg_keys[11], 71), 0),
        "v_resp": noise(arg_keys[9], (GROUPS, RTOK, KVH * DH), 1.0, 6.0, ((0, 8), (1, 4))),
        "g_resp": noise(arg_keys[10], (GROUPS, RTOK, HQ * DH), 1.0, 6.0, ((0, 8), (1, 4))),
    }


def attend(queries, keys_in, values_in, cotangent, allowed, live_rows):
    score_scale = DH ** -0.5
    row_count = queries.shape[0]
    key_count = keys_in.shape[0]
    heads_per = HQ // KVH
    masked_cot = jnp.where(live_rows[:, None], cotangent, jnp.zeros_like(cotangent))
    query_heads = queries.reshape(row_count, KVH, heads_per, DH).transpose(1, 0, 2, 3)
    cotan_heads = masked_cot.reshape(row_count, KVH, heads_per, DH).transpose(1, 0, 2, 3)
    key_heads = keys_in.reshape(key_count, KVH, DH).transpose(1, 0, 2)
    value_heads = values_in.reshape(key_count, KVH, DH).transpose(1, 0, 2)
    key_mask = allowed[None]
    live_cube = live_rows[:, None, None]

    def per_head(inputs):
        query_one, key_one, value_one, cotan_one = inputs
        query_f = query_one.astype(jnp.float32)
        key_f = key_one.astype(jnp.float32)
        value_f = value_one.astype(jnp.float32)
        cotan_f = cotan_one.astype(jnp.float32)
        scores = jnp.einsum("rgd,nd->grn", query_f, key_f) * score_scale
        row_top = jnp.max(jnp.where(key_mask, scores, -jnp.inf), axis=-1, keepdims=True)
        raised = jnp.where(key_mask, jnp.exp(scores - row_top), 0.0)
        softmax = raised / jnp.sum(raised, axis=-1, keepdims=True)
        soft_half = softmax.astype(jnp.bfloat16)
        mixed = jnp.einsum("grn,nd->rgd", soft_half.astype(jnp.float32), value_f)
        result = jnp.where(live_cube, mixed, 0.0).astype(jnp.bfloat16)
        row_delta = jnp.einsum("rgd,rgd->gr", cotan_f, result.astype(jnp.float32))
        dprob = jnp.einsum("rgd,nd->grn", cotan_f, value_f)
        dscore = (softmax * (dprob - row_delta[:, :, None]) * score_scale).astype(jnp.bfloat16)
        dscore_f = dscore.astype(jnp.float32)
        grad_query = jnp.einsum("grn,nd->rgd", dscore_f, key_f).astype(jnp.bfloat16)
        grad_key = jnp.einsum("grn,rgd->nd", dscore_f, query_f)
        grad_value = jnp.einsum("grn,rgd->nd", soft_half.astype(jnp.float32), cotan_f)
        return result, grad_query, grad_key, grad_value

    mixed_all, grad_q, grad_k, grad_v = lax.map(per_head, (query_heads, key_heads, value_heads, cotan_heads))
    return (mixed_all.transpose(1, 0, 2, 3).reshape(row_count, HQ * DH),
            grad_q.transpose(1, 0, 2, 3).reshape(row_count, HQ * DH),
            grad_k.transpose(1, 0, 2).reshape(key_count, KVH * DH),
            grad_v.transpose(1, 0, 2).reshape(key_count, KVH * DH))


def reference(prompt_len, resp_len, resp_host, q_prompt, k_prompt, v_prompt, g_prompt, q_resp, k_resp, v_resp, g_resp):
    key_index = jnp.arange(PROMPT, dtype=jnp.int32)

    def prompt_group(inputs):
        query_rows, key_rows, value_rows, cotan_rows, length = inputs
        allowed = (key_index[None, :] == key_index[:, None]) | ((key_index[None, :] < key_index[:, None]) & (key_index[:, None] < length))
        return attend(query_rows, key_rows, value_rows, cotan_rows, allowed, key_index < length)

    out_p, dq_p, dk_first, dv_first = lax.map(prompt_group, (q_prompt, k_prompt, v_prompt, g_prompt, prompt_len))
    device_total = GROUPS * N_SEQ
    q_dev = q_resp.reshape(device_total, R_SLOTS, HQ * DH)
    k_dev = k_resp.reshape(device_total, R_SLOTS, KVH * DH)
    v_dev = v_resp.reshape(device_total, R_SLOTS, KVH * DH)
    g_dev = g_resp.reshape(device_total, R_SLOTS, HQ * DH)
    group_ids = jnp.arange(GROUPS, dtype=jnp.int32)
    slot_index = jnp.arange(R_SLOTS, dtype=jnp.int32)

    def device_step(totals, inputs):
        acc_keys, acc_values = totals
        device_id, query_rows, key_rows, value_rows, cotan_rows = inputs
        group_id = device_id // N_SEQ
        shard_id = device_id % N_SEQ
        pair_slot = (group_id % 2) * N_SEQ + shard_id
        match_table = ((group_ids[:, None] // 2) == (group_id // 2)) & (resp_host == pair_slot)
        owner_id = jnp.sum(jnp.where(match_table, group_ids[:, None], 0)).astype(jnp.int32)
        resp_length = jnp.sum(jnp.where(match_table, resp_len, 0)).astype(jnp.int32)
        owner_length = prompt_len[owner_id]
        live_slots = slot_index < resp_length
        reach_prompt = live_slots[:, None] & (key_index[None, :] < owner_length)
        reach_resp = (slot_index[None, :] == slot_index[:, None]) | ((slot_index[None, :] < slot_index[:, None]) & live_slots[:, None])
        allowed = jnp.concatenate([reach_prompt, reach_resp], axis=1)
        keys_all = jnp.concatenate([k_prompt[owner_id], key_rows], axis=0)
        values_all = jnp.concatenate([v_prompt[owner_id], value_rows], axis=0)
        mixed, grad_q, grad_k, grad_v = attend(query_rows, keys_all, values_all, cotan_rows, allowed, live_slots)
        acc_keys = acc_keys.at[owner_id].add(grad_k[:PROMPT])
        acc_values = acc_values.at[owner_id].add(grad_v[:PROMPT])
        return (acc_keys, acc_values), (mixed, grad_q, grad_k[PROMPT:].astype(jnp.bfloat16), grad_v[PROMPT:].astype(jnp.bfloat16))

    zeros_acc = jnp.zeros((GROUPS, PROMPT, KVH * DH), jnp.float32)
    device_ids = jnp.arange(device_total, dtype=jnp.int32)
    (acc_keys, acc_values), (out_r, dq_r, dk_r, dv_r) = lax.scan(device_step, (zeros_acc, zeros_acc), (device_ids, q_dev, k_dev, v_dev, g_dev))
    dk_whole = (dk_first + acc_keys).astype(jnp.bfloat16)
    dv_whole = (dv_first + acc_values).astype(jnp.bfloat16)
    return (out_p, out_r.reshape(GROUPS, RTOK, HQ * DH), dq_p, dq_r.reshape(GROUPS, RTOK, HQ * DH),
            dk_whole, dv_whole, dk_r.reshape(GROUPS, RTOK, KVH * DH), dv_r.reshape(GROUPS, RTOK, KVH * DH))
```

```python
import jax
import jax.numpy as jnp
from jax import lax
from jax.experimental import pallas as pl
from jax.experimental.pallas import tpu as pltpu
from jax.sharding import PartitionSpec as P

HQ = 32
KVH = 4
DH = 128
PER = HQ // KVH
SCALE = DH ** (-0.5)
LOG2E = 1.4426950408889634
BLOCKED = -1e30
NN = (((1,), (0,)), ((), ()))
NT = (((1,), (1,)), ((), ()))
TN = (((0,), (0,)), ((), ()))


def dot(a, b, dims=NN):
    return lax.dot_general(a, b, dims, preferred_element_type=jnp.float32)


def swapped(block, axis, distance):
    count = lax.axis_size(axis)
    return lax.ppermute(block, axis, [(i, i ^ distance) for i in range(count)])


def tall(block):
    return jnp.concatenate([block[:, h * DH : (h + 1) * DH] for h in range(PER)], axis=0)


def wide(block):
    rows = block.shape[0] // PER
    return jnp.concatenate([block[h * rows : (h + 1) * rows] for h in range(PER)], axis=1)


def attend(queries, cotangent, keys, values, bias, live):
    rows, count = bias.shape
    scores = (dot(queries, keys, NT) * (SCALE * LOG2E)).reshape(PER, rows, count) + bias[None]
    top = jnp.max(scores, axis=-1, keepdims=True)
    raised = jnp.exp2(scores - top)
    total = jnp.sum(raised, axis=-1, keepdims=True)
    probs = (raised * (1.0 / total)).reshape(PER * rows, count)
    half = probs.astype(jnp.bfloat16)
    mixed = dot(half, values).reshape(PER, rows, DH)
    result = jnp.where(live[None], mixed, 0.0).astype(jnp.bfloat16).reshape(PER * rows, DH)
    delta = jnp.sum(
        cotangent.astype(jnp.float32) * result.astype(jnp.float32), axis=-1, keepdims=True
    )
    dprob = dot(cotangent, values, NT)
    dscore = (probs * (dprob - delta) * SCALE).astype(jnp.bfloat16)
    grad_q = dot(dscore, keys).astype(jnp.bfloat16)
    grad_k = dot(dscore, queries, TN)
    grad_v = dot(half, cotangent, TN)
    return result, grad_q, grad_k, grad_v


def kernel(count, *refs):
    facts, q_p, g_p, q_r, g_r, k_r, v_r = refs[:7]
    own_k = refs[7 : 7 + count]
    own_v = refs[7 + count : 7 + 2 * count]
    pair_k = refs[7 + 2 * count : 7 + 3 * count]
    pair_v = refs[7 + 3 * count : 7 + 4 * count]
    out_p, dq_p, out_r, dq_r, dk_r, dv_r, far, *near = refs[7 + 4 * count :]
    own_length, resp_length, owner_length, shard, is_own = [facts[i] for i in range(5)]
    is_own = is_own == 1
    piece = own_k[0].shape[0]
    rows = q_p.shape[0]
    slots = q_r.shape[0]
    span = count * piece
    column = lax.broadcasted_iota(jnp.int32, (1, span), 1)
    place = ((column // piece) ^ shard) * piece + column % piece
    position = lax.broadcasted_iota(jnp.int32, (rows, 1), 0) + shard * rows
    live = position < own_length
    allowed = (place == position) | ((place < position) & live)
    bias = jnp.where(allowed, 0.0, BLOCKED)
    keys = jnp.concatenate([ref[...] for ref in own_k], axis=0)
    values = jnp.concatenate([ref[...] for ref in own_v], axis=0)
    queries = tall(q_p[...])
    cotangent = tall(jnp.where(live, g_p[...], 0))
    result, grad_q, own_gk, own_gv = attend(queries, cotangent, keys, values, bias, live)
    out_p[...] = wide(result)
    dq_p[...] = wide(grad_q)

    slot = lax.broadcasted_iota(jnp.int32, (slots, 1), 0)
    live = slot < resp_length
    other = lax.broadcasted_iota(jnp.int32, (1, slots), 1)
    bias = jnp.concatenate(
        [
            jnp.where(live & (place < owner_length), 0.0, BLOCKED),
            jnp.where((other == slot) | ((other < slot) & live), 0.0, BLOCKED),
        ],
        axis=1,
    )
    keys = jnp.concatenate(
        [jnp.where(is_own, a[...], b[...]) for a, b in zip(own_k, pair_k)] + [k_r[...]], axis=0
    )
    values = jnp.concatenate(
        [jnp.where(is_own, a[...], b[...]) for a, b in zip(own_v, pair_v)] + [v_r[...]], axis=0
    )
    queries = tall(q_r[...])
    cotangent = tall(jnp.where(live, g_r[...], 0))
    result, grad_q, grad_k, grad_v = attend(queries, cotangent, keys, values, bias, live)
    out_r[...] = wide(result)
    dq_r[...] = wide(grad_q)
    dk_r[...] = grad_k[span:].astype(jnp.bfloat16)
    dv_r[...] = grad_v[span:].astype(jnp.bfloat16)
    for d in range(count):
        part = slice(d * piece, (d + 1) * piece)
        near[d][0] = own_gk[part] + jnp.where(is_own, grad_k[part], 0.0)
        near[d][1] = own_gv[part] + jnp.where(is_own, grad_v[part], 0.0)
        far[d, 0] = jnp.where(is_own, 0.0, grad_k[part]).astype(jnp.bfloat16)
        far[d, 1] = jnp.where(is_own, 0.0, grad_v[part]).astype(jnp.bfloat16)


def shards(
    prompt_len,
    resp_len,
    resp_host,
    q_prompt,
    k_prompt,
    v_prompt,
    g_prompt,
    q_resp,
    k_resp,
    v_resp,
    g_resp,
):
    group_id = lax.axis_index("grp")
    shard_id = lax.axis_index("seq")
    count = lax.axis_size("seq")
    rows = q_prompt.shape[1]
    slots = q_resp.shape[1]
    piece = k_prompt.shape[1]
    width = KVH * DH

    mine = jnp.concatenate([k_prompt[0], v_prompt[0]], axis=1)
    own = [mine] + [swapped(mine, "seq", d) for d in range(1, count)]
    pair = [swapped(part, "grp", 1) for part in own]

    group_ids = jnp.arange(prompt_len.shape[0], dtype=jnp.int32)
    own_length = jnp.sum(jnp.where(group_ids == group_id, prompt_len, 0))
    pair_slot = group_id % 2 * count + shard_id
    match = (group_ids[:, None] // 2 == group_id // 2) & (resp_host == pair_slot)
    owner = jnp.sum(jnp.where(match, group_ids[:, None], 0))
    resp_length = jnp.sum(jnp.where(match, resp_len, 0))
    owner_length = jnp.sum(jnp.where(group_ids == owner, prompt_len, 0))
    is_own = (owner == group_id).astype(jnp.int32)
    facts = jnp.stack([own_length, resp_length, owner_length, shard_id, is_own]).astype(jnp.int32)

    def block(height, lanes, offset=0):
        return pl.BlockSpec((height, lanes), lambda c: (0, c + offset))

    wide_p, wide_r = block(rows, PER * DH), block(slots, PER * DH)
    bf16 = jnp.bfloat16
    outs = pl.pallas_call(
        lambda *refs: kernel(count, *refs),
        grid=(KVH,),
        in_specs=[pl.BlockSpec(memory_space=pltpu.SMEM), wide_p, wide_p, wide_r, wide_r]
        + [block(slots, DH)] * 2
        + [block(piece, DH)] * count
        + [block(piece, DH, KVH)] * count
        + [block(piece, DH)] * count
        + [block(piece, DH, KVH)] * count,
        out_specs=[wide_p, wide_p, wide_r, wide_r]
        + [block(slots, DH)] * 2
        + [pl.BlockSpec((count, 2, piece, DH), lambda c: (0, 0, 0, c))]
        + [pl.BlockSpec((2, piece, DH), lambda c: (0, 0, c))] * count,
        out_shape=[jax.ShapeDtypeStruct((rows, HQ * DH), bf16)] * 2
        + [jax.ShapeDtypeStruct((slots, HQ * DH), bf16)] * 2
        + [jax.ShapeDtypeStruct((slots, width), bf16)] * 2
        + [jax.ShapeDtypeStruct((count, 2, piece, width), bf16)]
        + [jax.ShapeDtypeStruct((2, piece, width), jnp.float32)] * count,
        compiler_params=pltpu.CompilerParams(vmem_limit_bytes=56 * 2**20),
        name="tree_attention",
    )(facts, q_prompt[0], g_prompt[0], q_resp[0], g_resp[0], k_resp[0], v_resp[0], *own, *own, *pair, *pair)
    out_p, dq_p, out_r, dq_r, dk_r, dv_r, far, *near = outs
    back = swapped(far, "grp", 1)
    total = near[0] + back[0].astype(jnp.float32)
    for d in range(1, count):
        part = (near[d] + back[d].astype(jnp.float32)).astype(bf16)
        total = total + swapped(part, "seq", d).astype(jnp.float32)
    total = total.astype(bf16)
    return (
        out_p[None],
        out_r[None],
        dq_p[None],
        dq_r[None],
        total[0][None],
        total[1][None],
        dk_r[None],
        dv_r[None],
    )


def solution(mesh):
    split = P("grp", "seq", None)
    return jax.shard_map(
        shards,
        mesh=mesh,
        in_specs=(P(), P(), P()) + (split,) * 8,
        out_specs=(split,) * 8,
        check_vma=False,
    )
```

```python
import jax
import jax.numpy as jnp
from jax import lax
from jax.experimental import pallas as pl
from jax.experimental.pallas import tpu as pltpu
from jax.sharding import PartitionSpec as P

HQ = 32
KVH = 4
DH = 128
PER = HQ // KVH
SCALE = DH ** (-0.5)
LOG2E = 1.4426950408889634
BLOCKED = -1e30
LONG = 512
BF16 = jnp.bfloat16
F32 = jnp.float32
NN = (((1,), (0,)), ((), ()))
NT = (((1,), (1,)), ((), ()))
TN = (((0,), (0,)), ((), ()))


def dot(a, b, dims=NN):
    return lax.dot_general(a, b, dims, preferred_element_type=F32)


def swapped(block, axis, distance):
    count = lax.axis_size(axis)
    return lax.ppermute(block, axis, [(i, i ^ distance) for i in range(count)])


def tall(block):
    return jnp.concatenate([block[:, lanes(h)] for h in range(PER)], axis=0)


def wide(block):
    rows = block.shape[0] // PER
    return jnp.concatenate([block[h * rows : (h + 1) * rows] for h in range(PER)], axis=1)


def lanes(c, width=DH):
    return slice(c * width, (c + 1) * width)


def hosted(resp_len, resp_host, count):
    group = lax.axis_index("grp")
    first = group // 2 * 2
    slot = group % 2 * count + lax.axis_index("seq")
    owner, length = first, jnp.int32(0)
    for offset in range(2):
        for r in range(resp_host.shape[0]):
            match = resp_host[r, first + offset] == slot
            owner = jnp.where(match, first + offset, owner)
            length = jnp.where(match, resp_len[r, first + offset], length)
    return owner, length


def beside(a, b):
    blank = jnp.zeros_like(a)
    return jnp.concatenate(
        [jnp.concatenate([a, blank], axis=1), jnp.concatenate([jnp.zeros_like(b), b], axis=1)], axis=0
    )


def softmax(scores, dprob):
    top = jnp.max(scores, axis=-1, keepdims=True)
    raised = jnp.exp2(scores - top)
    probs = raised * (1.0 / jnp.sum(raised, axis=-1, keepdims=True))
    weighted = probs * dprob
    delta = jnp.sum(weighted, axis=-1, keepdims=True)
    return probs.astype(BF16), ((weighted - probs * delta) * SCALE).astype(BF16)


def masked(scores, bias):
    rows, columns = bias.shape
    scaled = (scores * (SCALE * LOG2E)).reshape(PER, rows, columns) + bias[None]
    return scaled.reshape(PER * rows, columns)


def prepare_kernel(
    count, prompt_table, len_table, host_table, q_p, g_p, q_r, g_r, k_r, v_r,
    qg_p, qg_r, bias_p, bias_r, own_r, keep_p, keep_r, chosen, buf_qp, buf_gp, buf_qr, buf_gr, buf_k, buf_v, prompt_len, resp_len, resp_host, sems,
):
    buffers = (buf_qr, buf_gr, buf_k, buf_v, buf_qp, buf_gp)
    copies = [
        pltpu.make_async_copy(src, dst, sems.at[i])
        for i, (src, dst) in enumerate(zip((q_r, g_r, k_r, v_r, q_p, g_p), buffers))
    ]
    tables = [
        pltpu.make_async_copy(src, dst, sems.at[6 + i])
        for i, (src, dst) in enumerate(
            ((prompt_table, prompt_len), (len_table, resp_len), (host_table, resp_host))
        )
    ]
    for copy in tables + copies:
        copy.start()
    for copy in tables:
        copy.wait()
    shard = lax.axis_index("seq")
    owner, resp_length = hosted(resp_len, resp_host, count)
    own_length = prompt_len[lax.axis_index("grp")]
    owner_length = prompt_len[owner]
    rows, slots = buf_qp.shape[0], buf_qr.shape[0]
    column = lax.broadcasted_iota(jnp.int32, (1, count * rows), 1)
    place = ((column // rows) ^ shard) * rows + column % rows
    position = lax.broadcasted_iota(jnp.int32, (rows, 1), 0) + shard * rows
    live_p = position < own_length
    bias_p[...] = jnp.where((place == position) | ((place < position) & live_p), 0.0, BLOCKED)
    slot = lax.broadcasted_iota(jnp.int32, (slots, 1), 0)
    live_r = slot < resp_length
    keep_p[...] = jnp.where(live_p, 1.0, 0.0) + jnp.zeros(keep_p.shape, F32)
    keep_r[...] = jnp.where(live_r, 1.0, 0.0) + jnp.zeros(keep_r.shape, F32)
    chosen[...] = jnp.zeros(chosen.shape, F32) + jnp.where(owner == lax.axis_index("grp"), 1.0, 0.0)
    bias_r[...] = jnp.where(live_r & (place < owner_length), 0.0, BLOCKED)
    other = lax.broadcasted_iota(jnp.int32, (1, slots), 1)
    bias_own = jnp.where((other == slot) | ((other < slot) & live_r), 0.0, BLOCKED)
    for copy in copies[:4]:
        copy.wait()
    for c in range(KVH):
        for h in range(PER):
            to, at = slice(h * slots, (h + 1) * slots), lanes(c * PER + h)
            qg_r[c, to, :DH] = buf_qr[:, at]
            qg_r[c, to, DH:] = jnp.where(live_r, buf_gr[:, at], 0)
        both = dot(qg_r[c], beside(buf_k[:, lanes(c)], buf_v[:, lanes(c)]), NT)
        for h in range(PER):
            to = slice(h * slots, (h + 1) * slots)
            own_r[c, to, :slots] = both[to, :slots] * (SCALE * LOG2E) + bias_own
            own_r[c, to, slots:] = both[to, slots:]
    for copy in copies[4:]:
        copy.wait()
    for c in range(KVH):
        for h in range(PER):
            to, at = slice(h * rows, (h + 1) * rows), lanes(c * PER + h)
            qg_p[c, to, :DH] = buf_qp[:, at]
            qg_p[c, to, DH:] = jnp.where(live_p, buf_gp[:, at], 0)


def response_kernel(count, *refs):
    qg, bias, own, chosen, k_r, v_r = refs[:6]
    own_kv, pair_kv = refs[6 : 6 + count], refs[6 + count : 6 + 2 * count]
    pds, mix, near, far, scores = refs[6 + 2 * count :]
    piece = own_kv[0].shape[0]
    span, slots = count * piece, k_r.shape[0]
    is_own = chosen[0:1, :]
    is_pair = 1.0 - is_own
    own_half, pair_half = is_own.astype(BF16), is_pair.astype(BF16)

    def first(c):
        for d in range(count):
            part = slice(d * piece, (d + 1) * piece)
            low = slice(span + 2 * slots + d * piece, span + 2 * slots + (d + 1) * piece)
            k = own_kv[d][:, lanes(c)] * own_half + pair_kv[d][:, lanes(c)] * pair_half
            v = own_kv[d][:, lanes(KVH + c)] * own_half + pair_kv[d][:, lanes(KVH + c)] * pair_half
            mix[c, part, :DH] = v
            mix[c, part, DH:] = jnp.zeros_like(v)
            mix[c, low, :DH] = jnp.zeros_like(k)
            mix[c, low, DH:] = k
        mix[c, span : span + 2 * slots] = beside(v_r[:, lanes(c)], k_r[:, lanes(c)])
        scores[c % 2, :, :span] = dot(qg[c, :, :DH], mix[c, span + 2 * slots :, DH:], NT)
        scores[c % 2, :, span:] = dot(qg[c, :, DH:], mix[c, :span, :DH], NT)

    def second(c):
        block = jnp.concatenate(
            [masked(scores[c % 2, :, :span], bias[...]), own[c, :, :slots]], axis=1
        )
        dprob = jnp.concatenate([scores[c % 2, :, span:], own[c, :, slots:]], axis=1)
        probs, dscore = softmax(block, dprob)
        pds[c, :, : span + slots] = probs
        pds[c, :, span + slots : span + 2 * slots] = dscore[:, span:]
        pds[c, :, span + 2 * slots :] = dscore[:, :span]

    def third(c):
        grad_k = dot(pds[c, :, span + 2 * slots :], qg[c, :, :DH], TN)
        grad_v = dot(pds[c, :, :span], qg[c, :, DH:], TN)
        for d in range(count):
            part = slice(d * piece, (d + 1) * piece)
            for i, grad in enumerate((grad_k[part], grad_v[part])):
                near[d, i, :, lanes(c)] = grad * is_own
                far[d, i, :, lanes(c)] = (grad * is_pair).astype(BF16)

    first(0)
    for c in range(KVH):
        if c + 1 < KVH:
            first(c + 1)
        second(c)
        third(c)


def prompt_kernel(count, qg, bias, near_r, *refs):
    own_kv = refs[:count]
    pds, mix, *near, scores = refs[count:]
    rows = piece = own_kv[0].shape[0]
    span = count * piece

    def first(c):
        for d in range(count):
            part, low = slice(d * piece, (d + 1) * piece), slice(span + d * piece, span + (d + 1) * piece)
            k, v = own_kv[d][:, lanes(c)], own_kv[d][:, lanes(KVH + c)]
            mix[c, part, :DH] = v
            mix[c, part, DH:] = jnp.zeros_like(v)
            mix[c, low, :DH] = jnp.zeros_like(k)
            mix[c, low, DH:] = k
        scores[c % 2, :, :span] = dot(qg[c, :, :DH], mix[c, span:, DH:], NT)
        scores[c % 2, :, span:] = dot(qg[c, :, DH:], mix[c, :span, :DH], NT)

    def second(c):
        probs, dscore = softmax(masked(scores[c % 2, :, :span], bias[...]), scores[c % 2, :, span:])
        pds[c, :, :span] = probs
        pds[c, :, span:] = dscore

    def third(c):
        grad_k = dot(pds[c, :, span:], qg[c, :, :DH], TN)
        grad_v = dot(pds[c, :, :span], qg[c, :, DH:], TN)
        for d in range(count):
            part = slice(d * piece, (d + 1) * piece)
            for i, grad in enumerate((grad_k[part], grad_v[part])):
                near[d][i, :, lanes(c)] = near_r[d, i, :, lanes(c)] + grad

    first(0)
    for c in range(KVH):
        if c + 1 < KVH:
            first(c + 1)
        second(c)
        third(c)


def kept(block, keep):
    rows = keep.shape[0]
    return (block.reshape(PER, rows, DH) * keep[None]).reshape(PER * rows, DH).astype(BF16)


def finish_kernel(span, keep_p, keep_r, pds_p, mix_p, pds_r, mix_r, qg_r, out_p, dq_p, out_r, dq_r, dk_r, dv_r):
    c = pl.program_id(0)
    slots = dk_r.shape[0]
    both = dot(pds_r[c], mix_r[c])
    out_r[...] = wide(kept(both[:, :DH], keep_r[...]))
    dq_r[...] = wide(both[:, DH:].astype(BF16))
    dv_r[...] = dot(pds_r[c, :, span : span + slots], qg_r[c, :, DH:], TN).astype(BF16)
    dk_r[...] = dot(pds_r[c, :, span + slots : span + 2 * slots], qg_r[c, :, :DH], TN).astype(BF16)
    both = dot(pds_p[c], mix_p[c])
    out_p[...] = wide(kept(both[:, :DH], keep_p[...]))
    dq_p[...] = wide(both[:, DH:].astype(BF16))


def attend(queries, cotangent, keys, values, bias, live):
    rows, count = bias.shape
    scores = (dot(queries, keys, NT) * (SCALE * LOG2E)).reshape(PER, rows, count) + bias[None]
    top = jnp.max(scores, axis=-1, keepdims=True)
    raised = jnp.exp2(scores - top)
    total = jnp.sum(raised, axis=-1, keepdims=True)
    probs = (raised * (1.0 / total)).reshape(PER * rows, count)
    half = probs.astype(BF16)
    mixed = dot(half, values).reshape(PER, rows, DH)
    result = jnp.where(live[None], mixed, 0.0).astype(BF16).reshape(PER * rows, DH)
    delta = jnp.sum(
        cotangent.astype(F32) * result.astype(F32), axis=-1, keepdims=True
    )
    dprob = dot(cotangent, values, NT)
    dscore = (probs * (dprob - delta) * SCALE).astype(BF16)
    grad_q = dot(dscore, keys).astype(BF16)
    grad_k = dot(dscore, queries, TN)
    grad_v = dot(half, cotangent, TN)
    return result, grad_q, grad_k, grad_v


def long_kernel(count, *refs):
    prompt_len, resp_len, resp_host, q_p, g_p, q_r, g_r, k_r, v_r = refs[:9]
    own_k, own_v, pair_k, pair_v = [refs[9 + i * count : 9 + (i + 1) * count] for i in range(4)]
    out_p, dq_p, out_r, dq_r, dk_r, dv_r, far, *near = refs[9 + 4 * count :]
    group = lax.axis_index("grp")
    shard = lax.axis_index("seq")
    own_length = prompt_len[group]
    owner, resp_length = hosted(resp_len, resp_host, count)
    owner_length = prompt_len[owner]
    is_own = owner == group
    piece = own_k[0].shape[0]
    rows = q_p.shape[0]
    slots = q_r.shape[0]
    span = count * piece
    column = lax.broadcasted_iota(jnp.int32, (1, span), 1)
    place = ((column // piece) ^ shard) * piece + column % piece
    position = lax.broadcasted_iota(jnp.int32, (rows, 1), 0) + shard * rows
    live = position < own_length
    allowed = (place == position) | ((place < position) & live)
    bias = jnp.where(allowed, 0.0, BLOCKED)
    keys = jnp.concatenate([ref[...] for ref in own_k], axis=0)
    values = jnp.concatenate([ref[...] for ref in own_v], axis=0)
    queries = tall(q_p[...])
    cotangent = tall(jnp.where(live, g_p[...], 0))
    result, grad_q, own_gk, own_gv = attend(queries, cotangent, keys, values, bias, live)
    out_p[...] = wide(result)
    dq_p[...] = wide(grad_q)

    slot = lax.broadcasted_iota(jnp.int32, (slots, 1), 0)
    live = slot < resp_length
    other = lax.broadcasted_iota(jnp.int32, (1, slots), 1)
    bias = jnp.concatenate(
        [
            jnp.where(live & (place < owner_length), 0.0, BLOCKED),
            jnp.where((other == slot) | ((other < slot) & live), 0.0, BLOCKED),
        ],
        axis=1,
    )
    keys = jnp.concatenate(
        [jnp.where(is_own, a[...], b[...]) for a, b in zip(own_k, pair_k)] + [k_r[...]], axis=0
    )
    values = jnp.concatenate(
        [jnp.where(is_own, a[...], b[...]) for a, b in zip(own_v, pair_v)] + [v_r[...]], axis=0
    )
    queries = tall(q_r[...])
    cotangent = tall(jnp.where(live, g_r[...], 0))
    result, grad_q, grad_k, grad_v = attend(queries, cotangent, keys, values, bias, live)
    out_r[...] = wide(result)
    dq_r[...] = wide(grad_q)
    dk_r[...] = grad_k[span:].astype(BF16)
    dv_r[...] = grad_v[span:].astype(BF16)
    for d in range(count):
        part = slice(d * piece, (d + 1) * piece)
        near[d][0] = own_gk[part] + jnp.where(is_own, grad_k[part], 0.0)
        near[d][1] = own_gv[part] + jnp.where(is_own, grad_v[part], 0.0)
        far[d, 0] = jnp.where(is_own, 0.0, grad_k[part]).astype(BF16)
        far[d, 1] = jnp.where(is_own, 0.0, grad_v[part]).astype(BF16)


def long_prompts(prompt_len, resp_len, resp_host, q_p, g_p, q_r, g_r, k_r, v_r, own, pair):
    count, rows, slots = len(own), q_p.shape[0], q_r.shape[0]
    piece, width = rows, KVH * DH

    def block(height, lanes, offset=0):
        return pl.BlockSpec((height, lanes), lambda c: (0, c + offset))

    wide_p, wide_r = block(rows, PER * DH), block(slots, PER * DH)
    return pl.pallas_call(
        lambda *refs: long_kernel(count, *refs),
        grid=(KVH,),
        in_specs=[pl.BlockSpec(memory_space=pltpu.SMEM)] * 3
        + [wide_p, wide_p, wide_r, wide_r]
        + [block(slots, DH)] * 2
        + [block(piece, DH)] * count
        + [block(piece, DH, KVH)] * count
        + [block(piece, DH)] * count
        + [block(piece, DH, KVH)] * count,
        out_specs=[wide_p, wide_p, wide_r, wide_r]
        + [block(slots, DH)] * 2
        + [pl.BlockSpec((count, 2, piece, DH), lambda c: (0, 0, 0, c))]
        + [pl.BlockSpec((2, piece, DH), lambda c: (0, 0, c))] * count,
        out_shape=[jax.ShapeDtypeStruct((rows, HQ * DH), BF16)] * 2
        + [jax.ShapeDtypeStruct((slots, HQ * DH), BF16)] * 2
        + [jax.ShapeDtypeStruct((slots, width), BF16)] * 2
        + [jax.ShapeDtypeStruct((count, 2, piece, width), BF16)]
        + [jax.ShapeDtypeStruct((2, piece, width), F32)] * count,
        compiler_params=pltpu.CompilerParams(vmem_limit_bytes=56 * 2**20),
        name="long_prompts",
    )(prompt_len, resp_len, resp_host, q_p, g_p, q_r, g_r, k_r, v_r, *own, *own, *pair, *pair)


def summed(near, back):
    total = near[0] + back[0].astype(F32)
    for d in range(1, len(near)):
        part = (near[d] + back[d].astype(F32)).astype(BF16)
        total = total + swapped(part, "seq", d).astype(F32)
    return total.astype(BF16)


def collected(out_p, dq_p, out_r, dq_r, dk_r, dv_r, total):
    return tuple(
        array[None] for array in (out_p, out_r, dq_p, dq_r, total[0], total[1], dk_r, dv_r)
    )


def shards(
    prompt_len,
    resp_len,
    resp_host,
    q_prompt,
    k_prompt,
    v_prompt,
    g_prompt,
    q_resp,
    k_resp,
    v_resp,
    g_resp,
):
    count = lax.axis_size("seq")
    rows = q_prompt.shape[1]
    slots = q_resp.shape[1]
    width = KVH * DH
    span = count * rows
    vmem, hbm = [pl.BlockSpec(memory_space=space) for space in (pltpu.VMEM, pltpu.HBM)]
    resp_len, resp_host = resp_len.T, resp_host.T

    def inside(*shape, dtype=BF16):
        return pltpu.VMEM(shape, dtype)

    def held(array):
        return pltpu.with_memory_space_constraint(array, pltpu.HBM)

    def options(megabytes):
        return pltpu.CompilerParams(vmem_limit_bytes=megabytes * 2**20)

    def cost(flops):
        return pl.CostEstimate(flops=flops, bytes_accessed=2**20, transcendentals=0)

    mine = jnp.concatenate([k_prompt[0], v_prompt[0]], axis=1)
    own = [mine] + [swapped(mine, "seq", d) for d in range(1, count)]
    if span > LONG:
        pair = [swapped(part, "grp", 1) for part in own]
        out_p, dq_p, out_r, dq_r, dk_r, dv_r, far, *near = long_prompts(
            prompt_len, resp_len, resp_host, q_prompt[0], g_prompt[0], q_resp[0], g_resp[0],
            k_resp[0], v_resp[0], own, pair,
        )
        total = summed(near, swapped(far, "grp", 1))
        return collected(out_p, dq_p, out_r, dq_r, dk_r, dv_r, total)

    qg_p, qg_r, bias_p, bias_r, own_r, keep_p, keep_r, chosen = pl.pallas_call(
        lambda *refs: prepare_kernel(count, *refs),
        in_specs=[hbm] * 9,
        out_specs=[vmem] * 8,
        out_shape=[
            inside(KVH, PER * rows, 2 * DH),
            inside(KVH, PER * slots, 2 * DH),
            inside(rows, span, dtype=F32),
            inside(slots, span, dtype=F32),
            inside(KVH, PER * slots, 2 * slots, dtype=F32),
            inside(rows, DH, dtype=F32),
            inside(slots, DH, dtype=F32),
            inside(8, DH, dtype=F32),
        ],
        scratch_shapes=[pltpu.VMEM((rows, HQ * DH), BF16)] * 2
        + [pltpu.VMEM((slots, HQ * DH), BF16)] * 2
        + [pltpu.VMEM((slots, width), BF16)] * 2
        + [pltpu.SMEM(t.shape, jnp.int32) for t in (prompt_len, resp_len, resp_host)]
        + [pltpu.SemaphoreType.DMA((9,))],
        compiler_params=options(20),
        cost_estimate=cost(4 * 10**9),
        name="prepare",
    )(
        held(prompt_len), held(resp_len), held(resp_host),
        held(q_prompt[0]), held(g_prompt[0]), held(q_resp[0]), held(g_resp[0]),
        held(k_resp[0]), held(v_resp[0]),
    )

    own[1:] = [lax.optimization_barrier((part, chosen))[0] for part in own[1:]]
    pair = [swapped(part, "grp", 1) for part in own]
    pds_r, mix_r, near_r, far = pl.pallas_call(
        lambda *refs: response_kernel(count, *refs),
        in_specs=[vmem] * (6 + 2 * count),
        out_specs=[vmem] * 4,
        out_shape=[
            inside(KVH, PER * slots, 2 * (span + slots)),
            inside(KVH, 2 * (span + slots), 2 * DH),
            inside(count, 2, rows, width, dtype=F32),
            inside(count, 2, rows, width),
        ],
        scratch_shapes=[pltpu.VMEM((2, PER * slots, 2 * span), F32)],
        compiler_params=options(20),
        cost_estimate=cost(3 * 10**9),
        name="responses",
    )(qg_r, bias_r, own_r, chosen, k_resp[0], v_resp[0], *own, *pair)
    back = swapped(far, "grp", 1)

    pds_p, mix_p, *near = pl.pallas_call(
        lambda *refs: prompt_kernel(count, *refs),
        in_specs=[vmem] * (3 + count),
        out_specs=[vmem] * (2 + count),
        out_shape=[inside(KVH, PER * rows, 2 * span), inside(KVH, 2 * span, 2 * DH)]
        + [inside(2, rows, width, dtype=F32)] * count,
        scratch_shapes=[pltpu.VMEM((2, PER * rows, 2 * span), F32)],
        compiler_params=options(20),
        cost_estimate=cost(2 * 10**9),
        name="prompts",
    )(qg_p, bias_p, near_r, *own)

    def block(height, extent):
        return pl.BlockSpec((height, extent), lambda c: (0, c))

    wide_p, wide_r = block(rows, PER * DH), block(slots, PER * DH)
    out_p, dq_p, out_r, dq_r, dk_r, dv_r = pl.pallas_call(
        lambda *refs: finish_kernel(span, *refs),
        grid=(KVH,),
        in_specs=[vmem] * 7,
        out_specs=[wide_p, wide_p, wide_r, wide_r] + [block(slots, DH)] * 2,
        out_shape=[jax.ShapeDtypeStruct((rows, HQ * DH), BF16)] * 2
        + [jax.ShapeDtypeStruct((slots, HQ * DH), BF16)] * 2
        + [jax.ShapeDtypeStruct((slots, width), BF16)] * 2,
        compiler_params=options(20),
        cost_estimate=cost(8 * 10**9),
        name="finish",
    )(keep_p, keep_r, pds_p, mix_p, pds_r, mix_r, qg_r)
    return collected(out_p, dq_p, out_r, dq_r, dk_r, dv_r, summed(near, back))


def solution(mesh):
    split = P("grp", "seq", None)
    return jax.shard_map(
        shards,
        mesh=mesh,
        in_specs=(P(), P(), P()) + (split,) * 8,
        out_specs=(split,) * 8,
        check_vma=False,
    )
```

```python
import jax
import jax.numpy as jnp
from jax import lax
from jax.experimental import pallas as pl
from jax.experimental.pallas import tpu as pltpu
from jax.sharding import PartitionSpec as P

HQ = 32
KVH = 4
DH = 128
PER = HQ // KVH
SCALE = DH ** (-0.5)
LOG2E = 1.4426950408889634
BLOCKED = -1e30
LONG = 512
BF16 = jnp.bfloat16
F32 = jnp.float32
NN = (((1,), (0,)), ((), ()))
NT = (((1,), (1,)), ((), ()))
TN = (((0,), (0,)), ((), ()))


def dot(a, b, dims=NN):
    return lax.dot_general(a, b, dims, preferred_element_type=F32)


def swapped(block, axis, distance):
    count = lax.axis_size(axis)
    return lax.ppermute(block, axis, [(i, i ^ distance) for i in range(count)])


def tall(block):
    return jnp.concatenate([block[:, lanes(h)] for h in range(PER)], axis=0)


def wide(block):
    rows = block.shape[0] // PER
    return jnp.concatenate([block[h * rows : (h + 1) * rows] for h in range(PER)], axis=1)


def lanes(c, width=DH):
    return slice(c * width, (c + 1) * width)


def hosted(resp_len, resp_host, count):
    group = lax.axis_index("grp")
    first = group // 2 * 2
    slot = group % 2 * count + lax.axis_index("seq")
    owner, length = first, jnp.int32(0)
    for offset in range(2):
        for r in range(resp_host.shape[0]):
            match = resp_host[r, first + offset] == slot
            owner = jnp.where(match, first + offset, owner)
            length = jnp.where(match, resp_len[r, first + offset], length)
    return owner, length


def beside(a, b):
    blank = jnp.zeros_like(a)
    return jnp.concatenate(
        [jnp.concatenate([a, blank], axis=1), jnp.concatenate([blank, b], axis=1)], axis=0
    )


def masked(scores, bias):
    return scores * (SCALE * LOG2E) + jnp.concatenate([bias] * (scores.shape[1] // DH), axis=1)


def prepare_kernel(
    count, prompt_table, len_table, host_table, q_p, g_p, q_r, g_r, k_r, v_r,
    qg_p, qg_r, bias_p, bias_r, own_e, own_d, own_s, keep_p, keep_r, chosen,
    buf_qp, buf_gp, buf_qr, buf_gr, buf_k, buf_v, prompt_len, resp_len, resp_host, sems,
):
    buffers = (buf_qr, buf_gr, buf_k, buf_v, buf_qp, buf_gp)
    copies = [
        pltpu.make_async_copy(src, dst, sems.at[i])
        for i, (src, dst) in enumerate(zip((q_r, g_r, k_r, v_r, q_p, g_p), buffers))
    ]
    tables = [
        pltpu.make_async_copy(src, dst, sems.at[6 + i])
        for i, (src, dst) in enumerate(
            ((prompt_table, prompt_len), (len_table, resp_len), (host_table, resp_host))
        )
    ]
    for copy in tables + copies:
        copy.start()
    for copy in tables:
        copy.wait()
    shard = lax.axis_index("seq")
    owner, resp_length = hosted(resp_len, resp_host, count)
    group = lax.axis_index("grp")
    own_length, owner_length = prompt_len[group], prompt_len[owner]
    rows, slots = buf_qp.shape[0], buf_qr.shape[0]
    span = count * rows
    key = lax.broadcasted_iota(jnp.int32, (span, DH), 0)
    place = ((key // rows) ^ shard) * rows + key % rows
    lane = lax.broadcasted_iota(jnp.int32, (span, DH), 1)
    bias_p[...] = jnp.where(place <= lane % rows + shard * rows, 0.0, BLOCKED)
    bias_r[...] = jnp.where(place < owner_length, 0.0, BLOCKED)
    key = lax.broadcasted_iota(jnp.int32, (slots, DH), 0)
    lane = lax.broadcasted_iota(jnp.int32, (slots, DH), 1)
    bias_own = jnp.where(key <= lane % slots, 0.0, BLOCKED)
    chosen[...] = jnp.zeros(chosen.shape, F32) + jnp.where(owner == group, 1.0, 0.0)
    lane = lax.broadcasted_iota(jnp.int32, keep_p.shape, 1)
    keep_p[...] = jnp.where(lane % rows + shard * rows < own_length, 1.0, 0.0)
    lane = lax.broadcasted_iota(jnp.int32, keep_r.shape, 1)
    keep_r[...] = jnp.where(lane % slots < resp_length, 1.0, 0.0)
    live_p = lax.broadcasted_iota(jnp.int32, (rows, 1), 0) + shard * rows < own_length
    live_r = lax.broadcasted_iota(jnp.int32, (slots, 1), 0) < resp_length
    for copy in copies[:4]:
        copy.wait()
    for c in range(KVH):
        for h in range(PER):
            to, at = slice(h * slots, (h + 1) * slots), lanes(c * PER + h)
            qg_r[c, to, :DH] = buf_qr[:, at]
            qg_r[c, to, DH:] = jnp.where(live_r, buf_gr[:, at], 0)
        both = dot(beside(buf_k[:, lanes(c)], buf_v[:, lanes(c)]), qg_r[c], NT)
        scores, dprob = masked(both[:slots], bias_own), both[slots:]
        top = jnp.max(scores, axis=0, keepdims=True)
        raised = jnp.exp2(scores - top)
        own_e[c] = raised
        own_d[c] = dprob
        own_s[c, 0:1] = top
        own_s[c, 1:2] = jnp.sum(raised, axis=0, keepdims=True)
        own_s[c, 2:3] = jnp.sum(raised * dprob, axis=0, keepdims=True)
    for copy in copies[4:]:
        copy.wait()
    for c in range(KVH):
        for h in range(PER):
            to, at = slice(h * rows, (h + 1) * rows), lanes(c * PER + h)
            qg_p[c, to, :DH] = buf_qp[:, at]
            qg_p[c, to, DH:] = jnp.where(live_p, buf_gp[:, at], 0)


def response_kernel(count, *refs):
    qg, bias, own_s, chosen = refs[:4]
    own_kv, pair_kv = refs[4 : 4 + count], refs[4 + count : 4 + 2 * count]
    probs_c, dscore_c, keys, values, own_t, near, far, scores = refs[4 + 2 * count :]
    piece = own_kv[0].shape[0]
    span = count * piece
    is_own = chosen[0:1, :]
    is_pair = 1.0 - is_own
    own_half, pair_half = is_own.astype(BF16), is_pair.astype(BF16)

    def first(c):
        for d in range(count):
            part = slice(d * piece, (d + 1) * piece)
            for to, at in ((keys, lanes(c)), (values, lanes(KVH + c))):
                to[c, part] = own_kv[d][:, at] * own_half + pair_kv[d][:, at] * pair_half
        scores[c % 2, :span] = dot(keys[c], qg[c, :, :DH], NT)
        scores[c % 2, span:] = dot(values[c], qg[c, :, DH:], NT)

    def second(c):
        block = masked(scores[c % 2, :span], bias[...])
        own_top = own_s[c, 0:1]
        top = jnp.maximum(jnp.max(block, axis=0, keepdims=True), own_top)
        raised = jnp.exp2(block - top)
        own_raised = jnp.exp2(own_top - top)
        total = jnp.sum(raised, axis=0, keepdims=True) + own_raised * own_s[c, 1:2]
        inverse = 1.0 / total
        probs = raised * inverse
        weighted = probs * scores[c % 2, span:]
        own_factor = own_raised * inverse
        delta = jnp.sum(weighted, axis=0, keepdims=True) + own_factor * own_s[c, 2:3]
        probs_c[c] = probs.astype(BF16)
        dscore_c[c] = ((weighted - probs * delta) * SCALE).astype(BF16)
        own_t[c, 0:1] = own_factor
        own_t[c, 1:2] = delta

    def third(c):
        grad_k = dot(dscore_c[c], qg[c, :, :DH])
        grad_v = dot(probs_c[c], qg[c, :, DH:])
        for d in range(count):
            part = slice(d * piece, (d + 1) * piece)
            for i, grad in enumerate((grad_k[part], grad_v[part])):
                near[d, i, :, lanes(c)] = grad * is_own
                far[d, i, :, lanes(c)] = (grad * is_pair).astype(BF16)

    first(0)
    for c in range(KVH):
        if c + 1 < KVH:
            first(c + 1)
        second(c)
        third(c)


def prompt_kernel(count, qg, bias, near_r, *refs):
    own_kv = refs[:count]
    probs_c, dscore_c, keys, values, *near, scores = refs[count:]
    piece = own_kv[0].shape[0]
    span = count * piece

    def first(c):
        for d in range(count):
            part = slice(d * piece, (d + 1) * piece)
            keys[c, part] = own_kv[d][:, lanes(c)]
            values[c, part] = own_kv[d][:, lanes(KVH + c)]
        scores[c % 2, :span] = dot(keys[c], qg[c, :, :DH], NT)
        scores[c % 2, span:] = dot(values[c], qg[c, :, DH:], NT)

    def second(c):
        block = masked(scores[c % 2, :span], bias[...])
        raised = jnp.exp2(block - jnp.max(block, axis=0, keepdims=True))
        probs = raised * (1.0 / jnp.sum(raised, axis=0, keepdims=True))
        weighted = probs * scores[c % 2, span:]
        delta = jnp.sum(weighted, axis=0, keepdims=True)
        probs_c[c] = probs.astype(BF16)
        dscore_c[c] = ((weighted - probs * delta) * SCALE).astype(BF16)

    def third(c):
        grad_k = dot(dscore_c[c], qg[c, :, :DH])
        grad_v = dot(probs_c[c], qg[c, :, DH:])
        for d in range(count):
            part = slice(d * piece, (d + 1) * piece)
            for i, grad in enumerate((grad_k[part], grad_v[part])):
                near[d][i, :, lanes(c)] = near_r[d, i, :, lanes(c)] + grad

    first(0)
    for c in range(KVH):
        if c + 1 < KVH:
            first(c + 1)
        second(c)
        third(c)


def finish_kernel(
    keep_p, probs_p, dscore_p, keys_p, values_p, keep_r, probs_c, dscore_c, keys_c, values_c,
    own_e, own_d, own_t, k_r, v_r, qg_r, out_p, dq_p, out_r, dq_r, dk_r, dv_r,
):
    c = pl.program_id(0)
    own_factor, delta = own_t[c, 0:1], own_t[c, 1:2]
    probs = own_e[c] * own_factor
    dscore = (probs * (own_d[c] - delta) * SCALE).astype(BF16)
    probs = probs.astype(BF16)
    dv_r[...] = dot(probs, qg_r[c, :, DH:]).astype(BF16)
    dk_r[...] = dot(dscore, qg_r[c, :, :DH]).astype(BF16)

    def across(block):
        return wide(block.astype(BF16).T)

    left = beside(values_c[c], keys_c[c])
    span = keys_c.shape[1]
    own = beside(v_r[...], k_r[...])
    left = jnp.concatenate([left[:span], own, left[span:]], axis=0)
    right = jnp.concatenate([probs_c[c], probs, dscore, dscore_c[c]], axis=0)
    both = dot(left, right, TN)
    out_r[...] = across(both[:DH] * keep_r[0:1])
    dq_r[...] = across(both[DH:])
    right = jnp.concatenate([probs_p[c], dscore_p[c]], axis=0)
    both = dot(beside(values_p[c], keys_p[c]), right, TN)
    out_p[...] = across(both[:DH] * keep_p[0:1])
    dq_p[...] = across(both[DH:])


def attend(queries, cotangent, keys, values, bias, live):
    rows, count = bias.shape
    scores = (dot(queries, keys, NT) * (SCALE * LOG2E)).reshape(PER, rows, count) + bias[None]
    top = jnp.max(scores, axis=-1, keepdims=True)
    raised = jnp.exp2(scores - top)
    total = jnp.sum(raised, axis=-1, keepdims=True)
    probs = (raised * (1.0 / total)).reshape(PER * rows, count)
    half = probs.astype(BF16)
    mixed = dot(half, values).reshape(PER, rows, DH)
    result = jnp.where(live[None], mixed, 0.0).astype(BF16).reshape(PER * rows, DH)
    delta = jnp.sum(
        cotangent.astype(F32) * result.astype(F32), axis=-1, keepdims=True
    )
    dprob = dot(cotangent, values, NT)
    dscore = (probs * (dprob - delta) * SCALE).astype(BF16)
    grad_q = dot(dscore, keys).astype(BF16)
    grad_k = dot(dscore, queries, TN)
    grad_v = dot(half, cotangent, TN)
    return result, grad_q, grad_k, grad_v


def long_kernel(count, *refs):
    prompt_len, resp_len, resp_host, q_p, g_p, q_r, g_r, k_r, v_r = refs[:9]
    own_k, own_v, pair_k, pair_v = [refs[9 + i * count : 9 + (i + 1) * count] for i in range(4)]
    out_p, dq_p, out_r, dq_r, dk_r, dv_r, far, *near = refs[9 + 4 * count :]
    group = lax.axis_index("grp")
    shard = lax.axis_index("seq")
    own_length = prompt_len[group]
    owner, resp_length = hosted(resp_len, resp_host, count)
    owner_length = prompt_len[owner]
    is_own = owner == group
    piece = own_k[0].shape[0]
    rows = q_p.shape[0]
    slots = q_r.shape[0]
    span = count * piece
    column = lax.broadcasted_iota(jnp.int32, (1, span), 1)
    place = ((column // piece) ^ shard) * piece + column % piece
    position = lax.broadcasted_iota(jnp.int32, (rows, 1), 0) + shard * rows
    live = position < own_length
    allowed = (place == position) | ((place < position) & live)
    bias = jnp.where(allowed, 0.0, BLOCKED)
    keys = jnp.concatenate([ref[...] for ref in own_k], axis=0)
    values = jnp.concatenate([ref[...] for ref in own_v], axis=0)
    queries = tall(q_p[...])
    cotangent = tall(jnp.where(live, g_p[...], 0))
    result, grad_q, own_gk, own_gv = attend(queries, cotangent, keys, values, bias, live)
    out_p[...] = wide(result)
    dq_p[...] = wide(grad_q)

    slot = lax.broadcasted_iota(jnp.int32, (slots, 1), 0)
    live = slot < resp_length
    other = lax.broadcasted_iota(jnp.int32, (1, slots), 1)
    bias = jnp.concatenate(
        [
            jnp.where(live & (place < owner_length), 0.0, BLOCKED),
            jnp.where((other == slot) | ((other < slot) & live), 0.0, BLOCKED),
        ],
        axis=1,
    )
    keys = jnp.concatenate(
        [jnp.where(is_own, a[...], b[...]) for a, b in zip(own_k, pair_k)] + [k_r[...]], axis=0
    )
    values = jnp.concatenate(
        [jnp.where(is_own, a[...], b[...]) for a, b in zip(own_v, pair_v)] + [v_r[...]], axis=0
    )
    queries = tall(q_r[...])
    cotangent = tall(jnp.where(live, g_r[...], 0))
    result, grad_q, grad_k, grad_v = attend(queries, cotangent, keys, values, bias, live)
    out_r[...] = wide(result)
    dq_r[...] = wide(grad_q)
    dk_r[...] = grad_k[span:].astype(BF16)
    dv_r[...] = grad_v[span:].astype(BF16)
    for d in range(count):
        part = slice(d * piece, (d + 1) * piece)
        near[d][0] = own_gk[part] + jnp.where(is_own, grad_k[part], 0.0)
        near[d][1] = own_gv[part] + jnp.where(is_own, grad_v[part], 0.0)
        far[d, 0] = jnp.where(is_own, 0.0, grad_k[part]).astype(BF16)
        far[d, 1] = jnp.where(is_own, 0.0, grad_v[part]).astype(BF16)


def long_prompts(prompt_len, resp_len, resp_host, q_p, g_p, q_r, g_r, k_r, v_r, own, pair):
    count, rows, slots = len(own), q_p.shape[0], q_r.shape[0]
    piece, width = rows, KVH * DH

    def block(height, lanes, offset=0):
        return pl.BlockSpec((height, lanes), lambda c: (0, c + offset))

    wide_p, wide_r = block(rows, PER * DH), block(slots, PER * DH)
    return pl.pallas_call(
        lambda *refs: long_kernel(count, *refs),
        grid=(KVH,),
        in_specs=[pl.BlockSpec(memory_space=pltpu.SMEM)] * 3
        + [wide_p, wide_p, wide_r, wide_r]
        + [block(slots, DH)] * 2
        + [block(piece, DH)] * count
        + [block(piece, DH, KVH)] * count
        + [block(piece, DH)] * count
        + [block(piece, DH, KVH)] * count,
        out_specs=[wide_p, wide_p, wide_r, wide_r]
        + [block(slots, DH)] * 2
        + [pl.BlockSpec((count, 2, piece, DH), lambda c: (0, 0, 0, c))]
        + [pl.BlockSpec((2, piece, DH), lambda c: (0, 0, c))] * count,
        out_shape=[jax.ShapeDtypeStruct((rows, HQ * DH), BF16)] * 2
        + [jax.ShapeDtypeStruct((slots, HQ * DH), BF16)] * 2
        + [jax.ShapeDtypeStruct((slots, width), BF16)] * 2
        + [jax.ShapeDtypeStruct((count, 2, piece, width), BF16)]
        + [jax.ShapeDtypeStruct((2, piece, width), F32)] * count,
        compiler_params=pltpu.CompilerParams(vmem_limit_bytes=56 * 2**20),
        name="long_prompts",
    )(prompt_len, resp_len, resp_host, q_p, g_p, q_r, g_r, k_r, v_r, *own, *own, *pair, *pair)


def summed(near, back):
    total = near[0] + back[0].astype(F32)
    for d in range(1, len(near)):
        part = (near[d] + back[d].astype(F32)).astype(BF16)
        total = total + swapped(part, "seq", d).astype(F32)
    return total.astype(BF16)


def collected(out_p, dq_p, out_r, dq_r, dk_r, dv_r, total):
    return tuple(
        array[None] for array in (out_p, out_r, dq_p, dq_r, total[0], total[1], dk_r, dv_r)
    )


def shards(
    prompt_len,
    resp_len,
    resp_host,
    q_prompt,
    k_prompt,
    v_prompt,
    g_prompt,
    q_resp,
    k_resp,
    v_resp,
    g_resp,
):
    count = lax.axis_size("seq")
    rows = q_prompt.shape[1]
    slots = q_resp.shape[1]
    width = KVH * DH
    span = count * rows
    vmem, hbm = [pl.BlockSpec(memory_space=space) for space in (pltpu.VMEM, pltpu.HBM)]
    resp_len, resp_host = resp_len.T, resp_host.T

    def inside(*shape, dtype=BF16):
        return pltpu.VMEM(shape, dtype)

    def held(array):
        return pltpu.with_memory_space_constraint(array, pltpu.HBM)

    def options(megabytes):
        return pltpu.CompilerParams(vmem_limit_bytes=megabytes * 2**20)

    def cost(flops):
        return pl.CostEstimate(flops=flops, bytes_accessed=2**20, transcendentals=0)

    mine = jnp.concatenate([k_prompt[0], v_prompt[0]], axis=1)
    own = [mine] + [swapped(mine, "seq", d) for d in range(1, count)]
    if span > LONG:
        pair = [swapped(part, "grp", 1) for part in own]
        out_p, dq_p, out_r, dq_r, dk_r, dv_r, far, *near = long_prompts(
            prompt_len, resp_len, resp_host, q_prompt[0], g_prompt[0], q_resp[0], g_resp[0],
            k_resp[0], v_resp[0], own, pair,
        )
        total = summed(near, swapped(far, "grp", 1))
        return collected(out_p, dq_p, out_r, dq_r, dk_r, dv_r, total)

    made = pl.pallas_call(
        lambda *refs: prepare_kernel(count, *refs),
        in_specs=[hbm] * 9,
        out_specs=[vmem] * 10,
        out_shape=[
            inside(KVH, PER * rows, 2 * DH),
            inside(KVH, PER * slots, 2 * DH),
            inside(span, DH, dtype=F32),
            inside(span, DH, dtype=F32),
            inside(KVH, slots, PER * slots, dtype=F32),
            inside(KVH, slots, PER * slots, dtype=F32),
            inside(KVH, 8, PER * slots, dtype=F32),
            inside(8, PER * rows, dtype=F32),
            inside(8, PER * slots, dtype=F32),
            inside(8, DH, dtype=F32),
        ],
        scratch_shapes=[pltpu.VMEM((rows, HQ * DH), BF16)] * 2
        + [pltpu.VMEM((slots, HQ * DH), BF16)] * 2
        + [pltpu.VMEM((slots, width), BF16)] * 2
        + [pltpu.SMEM(t.shape, jnp.int32) for t in (prompt_len, resp_len, resp_host)]
        + [pltpu.SemaphoreType.DMA((9,))],
        compiler_params=options(20),
        cost_estimate=cost(4 * 10**9),
        name="prepare",
    )(
        held(prompt_len), held(resp_len), held(resp_host),
        held(q_prompt[0]), held(g_prompt[0]), held(q_resp[0]), held(g_resp[0]),
        held(k_resp[0]), held(v_resp[0]),
    )
    qg_p, qg_r, bias_p, bias_r, own_e, own_d, own_s, keep_p, keep_r, chosen = made

    own[1:] = [lax.optimization_barrier((part, chosen))[0] for part in own[1:]]
    pair = [swapped(part, "grp", 1) for part in own]
    probs_c, dscore_c, keys_c, values_c, own_t, near_r, far = pl.pallas_call(
        lambda *refs: response_kernel(count, *refs),
        in_specs=[vmem] * (4 + 2 * count),
        out_specs=[vmem] * 7,
        out_shape=[inside(KVH, span, PER * slots)] * 2
        + [inside(KVH, span, DH)] * 2
        + [
            inside(KVH, 8, PER * slots, dtype=F32),
            inside(count, 2, rows, width, dtype=F32),
            inside(count, 2, rows, width),
        ],
        scratch_shapes=[pltpu.VMEM((2, 2 * span, PER * slots), F32)],
        compiler_params=options(20),
        cost_estimate=cost(3 * 10**9),
        name="responses",
    )(qg_r, bias_r, own_s, chosen, *own, *pair)
    back = swapped(far, "grp", 1)

    probs_p, dscore_p, keys_p, values_p, *near = pl.pallas_call(
        lambda *refs: prompt_kernel(count, *refs),
        in_specs=[vmem] * (3 + count),
        out_specs=[vmem] * (4 + count),
        out_shape=[inside(KVH, span, PER * rows)] * 2
        + [inside(KVH, span, DH)] * 2
        + [inside(2, rows, width, dtype=F32)] * count,
        scratch_shapes=[pltpu.VMEM((2, 2 * span, PER * rows), F32)],
        compiler_params=options(20),
        cost_estimate=cost(2 * 10**9),
        name="prompts",
    )(qg_p, bias_p, near_r, *own)

    def block(height, extent):
        return pl.BlockSpec((height, extent), lambda c: (0, c))

    wide_p, wide_r, own_block = block(rows, PER * DH), block(slots, PER * DH), block(slots, DH)
    out_p, dq_p, out_r, dq_r, dk_r, dv_r = pl.pallas_call(
        finish_kernel,
        grid=(KVH,),
        in_specs=[vmem] * 13 + [own_block] * 2 + [vmem],
        out_specs=[wide_p, wide_p, wide_r, wide_r, own_block, own_block],
        out_shape=[jax.ShapeDtypeStruct((rows, HQ * DH), BF16)] * 2
        + [jax.ShapeDtypeStruct((slots, HQ * DH), BF16)] * 2
        + [jax.ShapeDtypeStruct((slots, width), BF16)] * 2,
        compiler_params=options(20),
        cost_estimate=cost(8 * 10**9),
        name="finish",
    )(
        keep_p, probs_p, dscore_p, keys_p, values_p, keep_r, probs_c, dscore_c, keys_c, values_c,
        own_e, own_d, own_t, k_resp[0], v_resp[0], qg_r,
    )
    return collected(out_p, dq_p, out_r, dq_r, dk_r, dv_r, summed(near, back))


def solution(mesh):
    split = P("grp", "seq", None)
    return jax.shard_map(
        shards,
        mesh=mesh,
        in_specs=(P(), P(), P()) + (split,) * 8,
        out_specs=(split,) * 8,
        check_vma=False,
    )
```

```python
import jax
import jax.numpy as jnp
from jax import lax
from jax.experimental import pallas as pl
from jax.experimental.pallas import tpu as pltpu
from jax.sharding import PartitionSpec as P

HQ = 32
KVH = 4
DH = 128
PER = HQ // KVH
SCALE = DH ** (-0.5)
LOG2E = 1.4426950408889634
BLOCKED = -1e30
LONG = 512
ORDER = (3, 2, 1)
BF16 = jnp.bfloat16
F32 = jnp.float32
NN = (((1,), (0,)), ((), ()))
NT = (((1,), (1,)), ((), ()))
TN = (((0,), (0,)), ((), ()))


def dot(a, b, dims=NN):
    return lax.dot_general(a, b, dims, preferred_element_type=F32)


def swapped(block, axis, distance):
    count = lax.axis_size(axis)
    return lax.ppermute(block, axis, [(i, i ^ distance) for i in range(count)])


def tall(block):
    return jnp.concatenate([block[:, lanes(h)] for h in range(PER)], axis=0)


def wide(block):
    rows = block.shape[0] // PER
    return jnp.concatenate([block[h * rows : (h + 1) * rows] for h in range(PER)], axis=1)


def lanes(c, width=DH):
    return slice(c * width, (c + 1) * width)


def hosted(resp_len, resp_host, count):
    group = lax.axis_index("grp")
    first = group // 2 * 2
    slot = group % 2 * count + lax.axis_index("seq")
    owner, length = first, jnp.int32(0)
    for offset in range(2):
        for r in range(resp_host.shape[0]):
            match = resp_host[r, first + offset] == slot
            owner = jnp.where(match, first + offset, owner)
            length = jnp.where(match, resp_len[r, first + offset], length)
    return owner, length


def beside(a, b):
    blank = jnp.zeros_like(a)
    return jnp.concatenate(
        [jnp.concatenate([a, blank], axis=1), jnp.concatenate([blank, b], axis=1)], axis=0
    )


def prepare_kernel(
    count, prompt_table, len_table, host_table, q_p, g_p, q_r, g_r,
    qp_x, gp_x, gp_m, qr_x, gr_x, gr_m, mask_p, mask_r, mask_own, keep_p, keep_r, chosen,
    buf_qp, buf_gp, buf_qr, buf_gr, prompt_len, resp_len, resp_host, sems,
):
    buffers = (buf_qr, buf_gr, buf_qp, buf_gp)
    copies = [
        pltpu.make_async_copy(src, dst, sems.at[i])
        for i, (src, dst) in enumerate(zip((q_r, g_r, q_p, g_p), buffers))
    ]
    tables = [
        pltpu.make_async_copy(src, dst, sems.at[4 + i])
        for i, (src, dst) in enumerate(
            ((prompt_table, prompt_len), (len_table, resp_len), (host_table, resp_host))
        )
    ]
    for copy in tables + copies:
        copy.start()
    for copy in tables:
        copy.wait()
    shard = lax.axis_index("seq")
    owner, resp_length = hosted(resp_len, resp_host, count)
    group = lax.axis_index("grp")
    own_length, owner_length = prompt_len[group], prompt_len[owner]
    rows, slots = buf_qp.shape[0], buf_qr.shape[0]
    span = count * rows
    key = lax.broadcasted_iota(jnp.int32, (span, DH), 0)
    place = ((key // rows) ^ shard) * rows + key % rows
    lane = lax.broadcasted_iota(jnp.int32, (span, DH), 1)
    blocked_p = (place > lane + shard * rows) & (lane < rows)
    mask_p[...] = jnp.where(blocked_p, BLOCKED, 0.0).astype(BF16)
    mask_r[...] = jnp.where(place >= owner_length, BLOCKED, 0.0).astype(BF16)
    key = lax.broadcasted_iota(jnp.int32, (slots, DH), 0)
    lane = lax.broadcasted_iota(jnp.int32, (slots, DH), 1)
    mask_own[...] = jnp.where((key > lane) & (lane < slots), BLOCKED, 0.0).astype(BF16)
    hot_r = jnp.where(key == lane, 1.0, 0.0).astype(BF16)
    key = lax.broadcasted_iota(jnp.int32, (rows, DH), 0)
    lane = lax.broadcasted_iota(jnp.int32, (rows, DH), 1)
    hot_p = jnp.where(key == lane, 1.0, 0.0).astype(BF16)
    chosen[...] = jnp.zeros(chosen.shape, F32) + jnp.where(owner == group, 1.0, 0.0)
    lane = lax.broadcasted_iota(jnp.int32, keep_p.shape, 1)
    keep_p[...] = jnp.where(lane % rows + shard * rows < own_length, 1.0, 0.0)
    lane = lax.broadcasted_iota(jnp.int32, keep_r.shape, 1)
    keep_r[...] = jnp.where(lane % slots < resp_length, 1.0, 0.0)
    live_p = lax.broadcasted_iota(jnp.int32, (rows, 1), 0) + shard * rows < own_length
    live_r = lax.broadcasted_iota(jnp.int32, (slots, 1), 0) < resp_length
    def lay(c, height, q, g, live, hot, to_q, to_g, to_m):
        for h in range(PER):
            to, at = slice(h * height, (h + 1) * height), lanes(c * PER + h)
            to_q[c, to, :DH] = q[:, at]
            to_q[c, to, DH:] = hot
            kept = jnp.where(live, g[:, at], 0)
            to_m[c, to] = kept
            scaled = kept.astype(F32) * SCALE
            high = scaled.astype(BF16)
            to_g[c, to, :DH] = high
            to_g[c, to, DH:] = (scaled - high.astype(F32)).astype(BF16)

    for copy in copies[:2]:
        copy.wait()
    for c in range(KVH):
        lay(c, slots, buf_qr, buf_gr, live_r, hot_r, qr_x, gr_x, gr_m)
    for copy in copies[2:]:
        copy.wait()
    for c in range(KVH):
        lay(c, rows, buf_qp, buf_gp, live_p, hot_p, qp_x, gp_x, gp_m)


def in_turn(*stages):
    stages[0](0)
    for c in range(KVH):
        if c + 1 < KVH:
            stages[0](c + 1)
        for stage in stages[1:]:
            stage(c)


def chosen_pieces(chosen, own, pair, c, to, skip=0):
    own_half, pair_half = chosen[0:1, :].astype(BF16), (1.0 - chosen[0:1, :]).astype(BF16)
    piece = own[0].shape[0]
    for d in range(len(own)):
        to[c, d * piece : (d + 1) * piece] = (
            own[d][:, lanes(skip + c)] * own_half + pair[d][:, lanes(skip + c)] * pair_half
        )


def halves(block):
    return jnp.concatenate([block, block], axis=1)


def early_kernel(count, q_x, g_x, mask_r, mask_own, chosen, k_r, v_r, *refs):
    own, pair = refs[:count], refs[count : 2 * count]
    keys, values, raised_a, dprob_a, stats, scores = refs[2 * count :]
    span = keys.shape[1]

    def first(c):
        chosen_pieces(chosen, own, pair, c, keys)
        chosen_pieces(chosen, own, pair, c, values, KVH)
        key = jnp.concatenate([k_r[:, lanes(c)], keys[c]], axis=0)
        mask = jnp.concatenate([mask_own[...], mask_r[:span]], axis=0)
        value = jnp.concatenate([v_r[:, lanes(c)], values[c]], axis=0)
        scores[c % 2] = dot(jnp.concatenate([key, mask], axis=1), q_x[c], NT)
        dprob_a[c] = dot(halves(value), g_x[c], NT)

    def second(c):
        block = scores[c % 2] * (SCALE * LOG2E)
        top = jnp.max(block, axis=0, keepdims=True)
        raised = jnp.exp2(block - top)
        raised_a[c] = raised
        stats[c, 0:1] = top
        stats[c, 1:2] = jnp.sum(raised, axis=0, keepdims=True)
        stats[c, 2:3] = jnp.sum(raised * dprob_a[c], axis=0, keepdims=True)

    in_turn(first, second)


def response_kernel(count, q_x, g_x, g_m, mask_r, stats, raised_a, dprob_a, chosen, *refs):
    own, pair = refs[:count], refs[count : 2 * count]
    probs_c, dscore_c, keys, values, own_t, near, far, scores = refs[2 * count :]
    piece = own[0].shape[0]
    late = count * piece
    early = probs_c.shape[1] - late
    slots = raised_a.shape[1] - early
    is_own = chosen[0:1, :]
    is_pair = 1.0 - is_own

    def first(c):
        chosen_pieces(chosen, own, pair, c, keys)
        chosen_pieces(chosen, own, pair, c, values, KVH)
        scores[c % 2, :late] = dot(jnp.concatenate([keys[c], mask_r[early:]], axis=1), q_x[c], NT)
        scores[c % 2, late:] = dot(halves(values[c]), g_x[c], NT)

    def second(c):
        block = scores[c % 2, :late] * (SCALE * LOG2E)
        early_top = stats[c, 0:1]
        top = jnp.maximum(jnp.max(block, axis=0, keepdims=True), early_top)
        raised = jnp.exp2(block - top)
        early_raised = jnp.exp2(early_top - top)
        total = jnp.sum(raised, axis=0, keepdims=True) + early_raised * stats[c, 1:2]
        inverse = 1.0 / total
        factor = early_raised * inverse
        probs = raised * inverse
        weighted = probs * scores[c % 2, late:]
        delta = jnp.sum(weighted, axis=0, keepdims=True) + factor * stats[c, 2:3]
        probs_c[c, early:] = probs.astype(BF16)
        dscore_c[c, early:] = (weighted - probs * delta).astype(BF16)
        probs = raised_a[c, slots:] * factor
        probs_c[c, :early] = probs.astype(BF16)
        dscore_c[c, :early] = (probs * (dprob_a[c, slots:] - delta)).astype(BF16)
        own_t[c, 0:1] = factor
        own_t[c, 1:2] = delta

    def third(c):
        grad_k = dot(dscore_c[c], q_x[c, :, :DH])
        grad_v = dot(probs_c[c], g_m[c])
        for d in range((early + late) // piece):
            part = slice(d * piece, (d + 1) * piece)
            for i, grad in enumerate((grad_k[part], grad_v[part])):
                near[d, i, :, lanes(c)] = grad * is_own
                far[d, i, :, lanes(c)] = (grad * is_pair).astype(BF16)

    in_turn(first, second, third)


def prompt_probs_kernel(count, q_x, g_m, mask, *refs):
    own_kv = refs[:count]
    exact, probs_p, keys, near, scores = refs[count:]
    piece = own_kv[0].shape[0]

    def first(c):
        for d in range(count):
            keys[c, d * piece : (d + 1) * piece] = own_kv[d][:, lanes(c)]
        scores[c % 2] = dot(jnp.concatenate([keys[c], mask[...]], axis=1), q_x[c], NT)

    def second(c):
        block = scores[c % 2] * (SCALE * LOG2E)
        raised = jnp.exp2(block - jnp.max(block, axis=0, keepdims=True))
        probs = raised * (1.0 / jnp.sum(raised, axis=0, keepdims=True))
        exact[c] = probs
        probs_p[c] = probs.astype(BF16)

    def third(c):
        grad = dot(probs_p[c], g_m[c])
        for d in range(count):
            near[d, :, lanes(c)] = grad[d * piece : (d + 1) * piece]

    in_turn(first, second, third)


def prompt_grads_kernel(count, q_x, g_x, exact, near_v, near_r, *refs):
    own_kv = refs[:count]
    dscore_p, values, *near, dprob = refs[count:]
    piece = own_kv[0].shape[0]

    def first(c):
        for d in range(count):
            values[c, d * piece : (d + 1) * piece] = own_kv[d][:, lanes(KVH + c)]
        dprob[c % 2] = dot(jnp.concatenate([values[c], values[c]], axis=1), g_x[c], NT)

    def second(c):
        probs = exact[c]
        weighted = probs * dprob[c % 2]
        delta = jnp.sum(weighted, axis=0, keepdims=True)
        dscore_p[c] = (weighted - probs * delta).astype(BF16)

    def third(c):
        grad = dot(dscore_p[c], q_x[c, :, :DH])
        for d in range(count):
            part = grad[d * piece : (d + 1) * piece]
            near[d][0, :, lanes(c)] = near_r[d, 0, :, lanes(c)] + part
            near[d][1, :, lanes(c)] = near_r[d, 1, :, lanes(c)] + near_v[d, :, lanes(c)]

    in_turn(first, second, third)


def finish_kernel(
    keep_p, probs_p, dscore_p, keys_p, values_p, keep_r, probs_c, dscore_c, keys_a, values_a,
    keys_b, values_b, raised_a, dprob_a, own_t, k_r, v_r, q_x, g_m, out_p, dq_p, out_r, dq_r, dk_r, dv_r,
):
    c = pl.program_id(0)
    own_factor, delta = own_t[c, 0:1], own_t[c, 1:2]
    slots = k_r.shape[0]
    probs = raised_a[c, :slots] * own_factor
    dscore = (probs * (dprob_a[c, :slots] - delta)).astype(BF16)
    probs = probs.astype(BF16)
    dv_r[...] = dot(probs, g_m[c]).astype(BF16)
    dk_r[...] = dot(dscore, q_x[c, :, :DH]).astype(BF16)

    def across(block):
        return wide(block.astype(BF16).T)

    values = jnp.concatenate([values_a[c], values_b[c], v_r[...]], axis=0)
    keys = jnp.concatenate([k_r[...], keys_a[c], keys_b[c]], axis=0)
    left = beside(values, keys)
    right = jnp.concatenate([probs_c[c], probs, dscore, dscore_c[c]], axis=0)
    both = dot(left, right, TN)
    out_r[...] = across(both[:DH] * keep_r[0:1])
    dq_r[...] = across(both[DH:])
    right = jnp.concatenate([probs_p[c], dscore_p[c]], axis=0)
    both = dot(beside(values_p[c], keys_p[c]), right, TN)
    out_p[...] = across(both[:DH] * keep_p[0:1])
    dq_p[...] = across(both[DH:])


def attend(queries, cotangent, keys, values, bias, live):
    rows, count = bias.shape
    scores = (dot(queries, keys, NT) * (SCALE * LOG2E)).reshape(PER, rows, count) + bias[None]
    top = jnp.max(scores, axis=-1, keepdims=True)
    raised = jnp.exp2(scores - top)
    total = jnp.sum(raised, axis=-1, keepdims=True)
    probs = (raised * (1.0 / total)).reshape(PER * rows, count)
    half = probs.astype(BF16)
    mixed = dot(half, values).reshape(PER, rows, DH)
    result = jnp.where(live[None], mixed, 0.0).astype(BF16).reshape(PER * rows, DH)
    delta = jnp.sum(
        cotangent.astype(F32) * result.astype(F32), axis=-1, keepdims=True
    )
    dprob = dot(cotangent, values, NT)
    dscore = (probs * (dprob - delta) * SCALE).astype(BF16)
    grad_q = dot(dscore, keys).astype(BF16)
    grad_k = dot(dscore, queries, TN)
    grad_v = dot(half, cotangent, TN)
    return result, grad_q, grad_k, grad_v


def long_kernel(count, *refs):
    prompt_len, resp_len, resp_host, q_p, g_p, q_r, g_r, k_r, v_r = refs[:9]
    own_k, own_v, pair_k, pair_v = [refs[9 + i * count : 9 + (i + 1) * count] for i in range(4)]
    out_p, dq_p, out_r, dq_r, dk_r, dv_r, far, *near = refs[9 + 4 * count :]
    group = lax.axis_index("grp")
    shard = lax.axis_index("seq")
    own_length = prompt_len[group]
    owner, resp_length = hosted(resp_len, resp_host, count)
    owner_length = prompt_len[owner]
    is_own = owner == group
    piece = own_k[0].shape[0]
    rows = q_p.shape[0]
    slots = q_r.shape[0]
    span = count * piece
    column = lax.broadcasted_iota(jnp.int32, (1, span), 1)
    place = ((column // piece) ^ shard) * piece + column % piece
    position = lax.broadcasted_iota(jnp.int32, (rows, 1), 0) + shard * rows
    live = position < own_length
    allowed = (place == position) | ((place < position) & live)
    bias = jnp.where(allowed, 0.0, BLOCKED)
    keys = jnp.concatenate([ref[...] for ref in own_k], axis=0)
    values = jnp.concatenate([ref[...] for ref in own_v], axis=0)
    queries = tall(q_p[...])
    cotangent = tall(jnp.where(live, g_p[...], 0))
    result, grad_q, own_gk, own_gv = attend(queries, cotangent, keys, values, bias, live)
    out_p[...] = wide(result)
    dq_p[...] = wide(grad_q)

    slot = lax.broadcasted_iota(jnp.int32, (slots, 1), 0)
    live = slot < resp_length
    other = lax.broadcasted_iota(jnp.int32, (1, slots), 1)
    bias = jnp.concatenate(
        [
            jnp.where(live & (place < owner_length), 0.0, BLOCKED),
            jnp.where((other == slot) | ((other < slot) & live), 0.0, BLOCKED),
        ],
        axis=1,
    )
    keys = jnp.concatenate(
        [jnp.where(is_own, a[...], b[...]) for a, b in zip(own_k, pair_k)] + [k_r[...]], axis=0
    )
    values = jnp.concatenate(
        [jnp.where(is_own, a[...], b[...]) for a, b in zip(own_v, pair_v)] + [v_r[...]], axis=0
    )
    queries = tall(q_r[...])
    cotangent = tall(jnp.where(live, g_r[...], 0))
    result, grad_q, grad_k, grad_v = attend(queries, cotangent, keys, values, bias, live)
    out_r[...] = wide(result)
    dq_r[...] = wide(grad_q)
    dk_r[...] = grad_k[span:].astype(BF16)
    dv_r[...] = grad_v[span:].astype(BF16)
    for d in range(count):
        part = slice(d * piece, (d + 1) * piece)
        near[d][0] = own_gk[part] + jnp.where(is_own, grad_k[part], 0.0)
        near[d][1] = own_gv[part] + jnp.where(is_own, grad_v[part], 0.0)
        far[d, 0] = jnp.where(is_own, 0.0, grad_k[part]).astype(BF16)
        far[d, 1] = jnp.where(is_own, 0.0, grad_v[part]).astype(BF16)


def long_prompts(prompt_len, resp_len, resp_host, q_p, g_p, q_r, g_r, k_r, v_r, own, pair):
    count, rows, slots = len(own), q_p.shape[0], q_r.shape[0]
    piece, width = rows, KVH * DH

    def block(height, lanes, offset=0):
        return pl.BlockSpec((height, lanes), lambda c: (0, c + offset))

    wide_p, wide_r = block(rows, PER * DH), block(slots, PER * DH)
    return pl.pallas_call(
        lambda *refs: long_kernel(count, *refs),
        grid=(KVH,),
        in_specs=[pl.BlockSpec(memory_space=pltpu.SMEM)] * 3
        + [wide_p, wide_p, wide_r, wide_r]
        + [block(slots, DH)] * 2
        + [block(piece, DH)] * count
        + [block(piece, DH, KVH)] * count
        + [block(piece, DH)] * count
        + [block(piece, DH, KVH)] * count,
        out_specs=[wide_p, wide_p, wide_r, wide_r]
        + [block(slots, DH)] * 2
        + [pl.BlockSpec((count, 2, piece, DH), lambda c: (0, 0, 0, c))]
        + [pl.BlockSpec((2, piece, DH), lambda c: (0, 0, c))] * count,
        out_shape=[jax.ShapeDtypeStruct((rows, HQ * DH), BF16)] * 2
        + [jax.ShapeDtypeStruct((slots, HQ * DH), BF16)] * 2
        + [jax.ShapeDtypeStruct((slots, width), BF16)] * 2
        + [jax.ShapeDtypeStruct((count, 2, piece, width), BF16)]
        + [jax.ShapeDtypeStruct((2, piece, width), F32)] * count,
        compiler_params=pltpu.CompilerParams(vmem_limit_bytes=56 * 2**20),
        name="long_prompts",
    )(prompt_len, resp_len, resp_host, q_p, g_p, q_r, g_r, k_r, v_r, *own, *own, *pair, *pair)


def summed(near, back):
    parts = {}
    for d in range(1, len(near)):
        parts[d] = swapped((near[d] + back[d].astype(F32)).astype(BF16), "seq", d)
    total = near[0] + back[0].astype(F32)
    for d in ORDER if len(near) == 4 else parts:
        total = total + parts[d].astype(F32)
    return total.astype(BF16)


def collected(out_p, dq_p, out_r, dq_r, dk_r, dv_r, total):
    return tuple(
        array[None] for array in (out_p, out_r, dq_p, dq_r, total[0], total[1], dk_r, dv_r)
    )


def shards(
    prompt_len,
    resp_len,
    resp_host,
    q_prompt,
    k_prompt,
    v_prompt,
    g_prompt,
    q_resp,
    k_resp,
    v_resp,
    g_resp,
):
    count = lax.axis_size("seq")
    rows = q_prompt.shape[1]
    slots = q_resp.shape[1]
    width = KVH * DH
    span = count * rows
    vmem, hbm = [pl.BlockSpec(memory_space=space) for space in (pltpu.VMEM, pltpu.HBM)]
    resp_len, resp_host = resp_len.T, resp_host.T

    def inside(*shape, dtype=BF16):
        return pltpu.VMEM(shape, dtype)

    def held(array):
        return pltpu.with_memory_space_constraint(array, pltpu.HBM)

    def options(megabytes):
        return pltpu.CompilerParams(vmem_limit_bytes=megabytes * 2**20)

    def cost(flops):
        return pl.CostEstimate(flops=flops, bytes_accessed=2**20, transcendentals=0)

    mine = jnp.concatenate([k_prompt[0], v_prompt[0]], axis=1)
    own = [mine] + [swapped(mine, "seq", d) for d in range(1, count)]
    if span > LONG or max(rows, slots) > DH:
        pair = [swapped(part, "grp", 1) for part in own]
        out_p, dq_p, out_r, dq_r, dk_r, dv_r, far, *near = long_prompts(
            prompt_len, resp_len, resp_host, q_prompt[0], g_prompt[0], q_resp[0], g_resp[0],
            k_resp[0], v_resp[0], own, pair,
        )
        total = summed(near, swapped(far, "grp", 1))
        return collected(out_p, dq_p, out_r, dq_r, dk_r, dv_r, total)

    made = pl.pallas_call(
        lambda *refs: prepare_kernel(count, *refs),
        in_specs=[hbm] * 7,
        out_specs=[vmem] * 12,
        out_shape=[inside(KVH, PER * rows, 2 * DH)] * 2
        + [inside(KVH, PER * rows, DH)]
        + [inside(KVH, PER * slots, 2 * DH)] * 2
        + [inside(KVH, PER * slots, DH)]
        + [inside(span, DH)] * 2
        + [
            inside(slots, DH),
            inside(8, PER * rows, dtype=F32),
            inside(8, PER * slots, dtype=F32),
            inside(8, DH, dtype=F32),
        ],
        scratch_shapes=[pltpu.VMEM((rows, HQ * DH), BF16)] * 2
        + [pltpu.VMEM((slots, HQ * DH), BF16)] * 2
        + [pltpu.SMEM(t.shape, jnp.int32) for t in (prompt_len, resp_len, resp_host)]
        + [pltpu.SemaphoreType.DMA((7,))],
        compiler_params=options(20),
        cost_estimate=cost(4 * 10**9),
        name="prepare",
    )(
        held(prompt_len), held(resp_len), held(resp_host),
        held(q_prompt[0]), held(g_prompt[0]), held(q_resp[0]), held(g_resp[0]),
    )
    qp_x, gp_x, gp_m, qr_x, gr_x, gr_m, mask_p, mask_r, mask_own, *rest = made
    keep_p, keep_r, chosen = rest

    here = 1
    pair = [swapped(part, "grp", 1) for part in own[:here]]
    keys_a, values_a, raised_a, dprob_a, stats = pl.pallas_call(
        lambda *refs: early_kernel(here, *refs),
        in_specs=[vmem] * (7 + 2 * here),
        out_specs=[vmem] * 5,
        out_shape=[inside(KVH, here * rows, DH)] * 2
        + [inside(KVH, slots + here * rows, PER * slots, dtype=F32)] * 2
        + [inside(KVH, 8, PER * slots, dtype=F32)],
        scratch_shapes=[pltpu.VMEM((2, slots + here * rows, PER * slots), F32)],
        compiler_params=options(16),
        cost_estimate=cost(3 * 10**9),
        name="early",
    )(qr_x, gr_x, mask_r, mask_own, chosen, k_resp[0], v_resp[0], *own[:here], *pair)
    own[here:] = [lax.optimization_barrier((part, stats))[0] for part in own[here:]]
    pair += [swapped(part, "grp", 1) for part in own[here:]]

    exact, probs_p, keys_p, near_v = pl.pallas_call(
        lambda *refs: prompt_probs_kernel(count, *refs),
        in_specs=[vmem] * (3 + count),
        out_specs=[vmem] * 4,
        out_shape=[
            inside(KVH, span, PER * rows, dtype=F32),
            inside(KVH, span, PER * rows),
            inside(KVH, span, DH),
            inside(count, rows, width, dtype=F32),
        ],
        scratch_shapes=[pltpu.VMEM((2, span, PER * rows), F32)],
        compiler_params=options(12),
        cost_estimate=cost(2 * 10**9),
        name="prompt_probs",
    )(qp_x, gp_m, mask_p, *own)

    stats, near_v = lax.optimization_barrier((stats, near_v))
    late = count - here
    probs_c, dscore_c, keys_b, values_b, own_t, near_r, far = pl.pallas_call(
        lambda *refs: response_kernel(late, *refs),
        in_specs=[vmem] * (8 + 2 * late),
        out_specs=[vmem] * 7,
        out_shape=[inside(KVH, span, PER * slots)] * 2
        + [inside(KVH, late * rows, DH)] * 2
        + [
            inside(KVH, 8, PER * slots, dtype=F32),
            inside(count, 2, rows, width, dtype=F32),
            inside(count, 2, rows, width),
        ],
        scratch_shapes=[pltpu.VMEM((2, 2 * late * rows, PER * slots), F32)],
        compiler_params=options(20),
        cost_estimate=cost(3 * 10**9),
        name="responses",
    )(
        qr_x, gr_x, gr_m, mask_r, stats, raised_a, dprob_a, chosen, *own[here:], *pair[here:]
    )
    back = swapped(far, "grp", 1)

    dscore_p, values_p, *near = pl.pallas_call(
        lambda *refs: prompt_grads_kernel(count, *refs),
        in_specs=[vmem] * (5 + count),
        out_specs=[vmem] * (2 + count),
        out_shape=[inside(KVH, span, PER * rows), inside(KVH, span, DH)]
        + [inside(2, rows, width, dtype=F32)] * count,
        scratch_shapes=[pltpu.VMEM((2, span, PER * rows), F32)],
        compiler_params=options(12),
        cost_estimate=cost(2 * 10**9),
        name="prompt_grads",
    )(qp_x, gp_x, exact, near_v, near_r, *own)

    def block(height, extent):
        return pl.BlockSpec((height, extent), lambda c: (0, c))

    wide_p, wide_r, own_block = block(rows, PER * DH), block(slots, PER * DH), block(slots, DH)
    out_p, dq_p, out_r, dq_r, dk_r, dv_r = pl.pallas_call(
        finish_kernel,
        grid=(KVH,),
        in_specs=[vmem] * 15 + [own_block] * 2 + [vmem] * 2,
        out_specs=[wide_p, wide_p, wide_r, wide_r, own_block, own_block],
        out_shape=[jax.ShapeDtypeStruct((rows, HQ * DH), BF16)] * 2
        + [jax.ShapeDtypeStruct((slots, HQ * DH), BF16)] * 2
        + [jax.ShapeDtypeStruct((slots, width), BF16)] * 2,
        compiler_params=options(20),
        cost_estimate=cost(8 * 10**9),
        name="finish",
    )(
        keep_p, probs_p, dscore_p, keys_p, values_p, keep_r, probs_c, dscore_c, keys_a, values_a,
        keys_b, values_b, raised_a, dprob_a, own_t, k_resp[0], v_resp[0], qr_x, gr_m,
    )
    return collected(out_p, dq_p, out_r, dq_r, dk_r, dv_r, summed(near, back))


def solution(mesh):
    split = P("grp", "seq", None)
    return jax.shard_map(
        shards,
        mesh=mesh,
        in_specs=(P(), P(), P()) + (split,) * 8,
        out_specs=(split,) * 8,
        check_vma=False,
    )
```

```python
import jax
import jax.numpy as jnp
from jax import lax
from jax.experimental import pallas as pl
from jax.experimental.pallas import tpu as pltpu
from jax.sharding import PartitionSpec as P

HQ = 32
KVH = 4
DH = 128
PER = HQ // KVH
SCALE = DH ** (-0.5)
LOG2E = 1.4426950408889634
BLOCKED = -1e30
LONG = 512
ORDER = (3, 2, 1)
BF16 = jnp.bfloat16
F32 = jnp.float32
NN = (((1,), (0,)), ((), ()))
NT = (((1,), (1,)), ((), ()))
TN = (((0,), (0,)), ((), ()))


def dot(a, b, dims=NN):
    return lax.dot_general(a, b, dims, preferred_element_type=F32)


def swapped(block, axis, distance):
    count = lax.axis_size(axis)
    return lax.ppermute(block, axis, [(i, i ^ distance) for i in range(count)])


def tall(block):
    return jnp.concatenate([block[:, lanes(h)] for h in range(PER)], axis=0)


def wide(block):
    rows = block.shape[0] // PER
    return jnp.concatenate([block[h * rows : (h + 1) * rows] for h in range(PER)], axis=1)


def lanes(c, width=DH):
    return slice(c * width, (c + 1) * width)


def hosted(resp_len, resp_host, count):
    group = lax.axis_index("grp")
    first = group // 2 * 2
    slot = group % 2 * count + lax.axis_index("seq")
    owner, length = first, jnp.int32(0)
    for offset in range(2):
        for r in range(resp_host.shape[0]):
            match = resp_host[r, first + offset] == slot
            owner = jnp.where(match, first + offset, owner)
            length = jnp.where(match, resp_len[r, first + offset], length)
    return owner, length


def beside(a, b):
    blank = jnp.zeros_like(a)
    return jnp.concatenate(
        [jnp.concatenate([a, blank], axis=1), jnp.concatenate([blank, b], axis=1)], axis=0
    )


def prepare_kernel(
    count, prompt_table, len_table, host_table, q_p, g_p, q_r, g_r,
    qp_x, gp_x, gp_m, qr_x, gr_x, gr_m, mask_p, mask_r, mask_own, keep_p, keep_r, chosen,
    buf_qp, buf_gp, buf_qr, buf_gr, prompt_len, resp_len, resp_host, sems,
):
    buffers = (buf_qr, buf_gr, buf_qp, buf_gp)
    copies = [
        pltpu.make_async_copy(src, dst, sems.at[i])
        for i, (src, dst) in enumerate(zip((q_r, g_r, q_p, g_p), buffers))
    ]
    tables = [
        pltpu.make_async_copy(src, dst, sems.at[4 + i])
        for i, (src, dst) in enumerate(
            ((prompt_table, prompt_len), (len_table, resp_len), (host_table, resp_host))
        )
    ]
    for copy in tables + copies:
        copy.start()
    for copy in tables:
        copy.wait()
    shard = lax.axis_index("seq")
    owner, resp_length = hosted(resp_len, resp_host, count)
    group = lax.axis_index("grp")
    own_length, owner_length = prompt_len[group], prompt_len[owner]
    rows, slots = buf_qp.shape[0], buf_qr.shape[0]
    span = count * rows
    key = lax.broadcasted_iota(jnp.int32, (span, DH), 0)
    place = ((key // rows) ^ shard) * rows + key % rows
    lane = lax.broadcasted_iota(jnp.int32, (span, DH), 1)
    blocked_p = (place > lane + shard * rows) & (lane < rows)
    mask_p[...] = jnp.where(blocked_p, BLOCKED, 0.0).astype(BF16)
    mask_r[...] = jnp.where(place >= owner_length, BLOCKED, 0.0).astype(BF16)
    key = lax.broadcasted_iota(jnp.int32, (slots, DH), 0)
    lane = lax.broadcasted_iota(jnp.int32, (slots, DH), 1)
    mask_own[...] = jnp.where((key > lane) & (lane < slots), BLOCKED, 0.0).astype(BF16)
    hot_r = jnp.where(key == lane, 1.0, 0.0).astype(BF16)
    key = lax.broadcasted_iota(jnp.int32, (rows, DH), 0)
    lane = lax.broadcasted_iota(jnp.int32, (rows, DH), 1)
    hot_p = jnp.where(key == lane, 1.0, 0.0).astype(BF16)
    chosen[...] = jnp.zeros(chosen.shape, F32) + jnp.where(owner == group, 1.0, 0.0)
    lane = lax.broadcasted_iota(jnp.int32, keep_p.shape, 1)
    keep_p[...] = jnp.where(lane % rows + shard * rows < own_length, 1.0, 0.0)
    lane = lax.broadcasted_iota(jnp.int32, keep_r.shape, 1)
    keep_r[...] = jnp.where(lane % slots < resp_length, 1.0, 0.0)
    live_p = lax.broadcasted_iota(jnp.int32, (rows, 1), 0) + shard * rows < own_length
    live_r = lax.broadcasted_iota(jnp.int32, (slots, 1), 0) < resp_length
    def lay(c, height, q, g, live, hot, to_q, to_g, to_m):
        for h in range(PER):
            to, at = slice(h * height, (h + 1) * height), lanes(c * PER + h)
            to_q[c, to, :DH] = q[:, at]
            to_q[c, to, DH:] = hot
            kept = jnp.where(live, g[:, at], 0)
            to_m[c, to] = kept
            scaled = kept.astype(F32) * SCALE
            high = scaled.astype(BF16)
            to_g[c, to, :DH] = high
            to_g[c, to, DH:] = (scaled - high.astype(F32)).astype(BF16)

    for copy in copies[:2]:
        copy.wait()
    for c in range(KVH):
        lay(c, slots, buf_qr, buf_gr, live_r, hot_r, qr_x, gr_x, gr_m)
    for copy in copies[2:]:
        copy.wait()
    for c in range(KVH):
        lay(c, rows, buf_qp, buf_gp, live_p, hot_p, qp_x, gp_x, gp_m)


def in_turn(*stages):
    stages[0](0)
    for c in range(KVH):
        if c + 1 < KVH:
            stages[0](c + 1)
        for stage in stages[1:]:
            stage(c)


def chosen_pieces(chosen, own, pair, c, to, skip=0):
    own_half, pair_half = chosen[0:1, :].astype(BF16), (1.0 - chosen[0:1, :]).astype(BF16)
    piece = own[0].shape[0]
    for d in range(len(own)):
        to[c, d * piece : (d + 1) * piece] = (
            own[d][:, lanes(skip + c)] * own_half + pair[d][:, lanes(skip + c)] * pair_half
        )


def halves(block):
    return jnp.concatenate([block, block], axis=1)


def early_kernel(count, q_x, g_x, mask_r, mask_own, chosen, k_r, v_r, *refs):
    own, pair = refs[:count], refs[count : 2 * count]
    keys, values, raised_a, dprob_a, stats, scores = refs[2 * count :]
    span = keys.shape[1]

    def first(c):
        chosen_pieces(chosen, own, pair, c, keys)
        chosen_pieces(chosen, own, pair, c, values, KVH)
        key = jnp.concatenate([k_r[:, lanes(c)], keys[c]], axis=0)
        mask = jnp.concatenate([mask_own[...], mask_r[:span]], axis=0)
        value = jnp.concatenate([v_r[:, lanes(c)], values[c]], axis=0)
        scores[c % 2] = dot(jnp.concatenate([key, mask], axis=1), q_x[c], NT)
        dprob_a[c] = dot(halves(value), g_x[c], NT)

    def second(c):
        block = scores[c % 2] * (SCALE * LOG2E)
        top = jnp.max(block, axis=0, keepdims=True)
        raised = jnp.exp2(block - top)
        raised_a[c] = raised
        stats[c, 0:1] = top
        stats[c, 1:2] = jnp.sum(raised, axis=0, keepdims=True)
        stats[c, 2:3] = jnp.sum(raised * dprob_a[c], axis=0, keepdims=True)

    in_turn(first, second)


def response_kernel(count, q_x, g_x, g_m, mask_r, stats, chosen, *refs):
    own, pair = refs[:count], refs[count : 2 * count]
    probs_c, dscore_c, keys, values, own_t, near, far, scores = refs[2 * count :]
    piece = own[0].shape[0]
    late = count * piece
    early = mask_r.shape[0] - late
    is_own = chosen[0:1, :]
    is_pair = 1.0 - is_own

    def first(c):
        chosen_pieces(chosen, own, pair, c, keys)
        chosen_pieces(chosen, own, pair, c, values, KVH)
        scores[c % 2, :late] = dot(jnp.concatenate([keys[c], mask_r[early:]], axis=1), q_x[c], NT)
        scores[c % 2, late:] = dot(halves(values[c]), g_x[c], NT)

    def second(c):
        block = scores[c % 2, :late] * (SCALE * LOG2E)
        early_top = stats[c, 0:1]
        top = jnp.maximum(jnp.max(block, axis=0, keepdims=True), early_top)
        raised = jnp.exp2(block - top)
        early_raised = jnp.exp2(early_top - top)
        total = jnp.sum(raised, axis=0, keepdims=True) + early_raised * stats[c, 1:2]
        inverse = 1.0 / total
        factor = early_raised * inverse
        probs = raised * inverse
        weighted = probs * scores[c % 2, late:]
        delta = jnp.sum(weighted, axis=0, keepdims=True) + factor * stats[c, 2:3]
        probs_c[c] = probs.astype(BF16)
        dscore_c[c] = (weighted - probs * delta).astype(BF16)
        own_t[c, 0:1] = factor
        own_t[c, 1:2] = delta

    def third(c):
        grad_k = dot(dscore_c[c], q_x[c, :, :DH])
        grad_v = dot(probs_c[c], g_m[c])
        for d in range(count):
            part = slice(d * piece, (d + 1) * piece)
            for i, grad in enumerate((grad_k[part], grad_v[part])):
                near[d, i, :, lanes(c)] = grad * is_own
                far[d, i, :, lanes(c)] = (grad * is_pair).astype(BF16)

    in_turn(first, second, third)


def prompt_probs_kernel(count, q_x, g_m, mask, *refs):
    own_kv = refs[:count]
    exact, probs_p, keys, near, scores = refs[count:]
    piece = own_kv[0].shape[0]

    def first(c):
        for d in range(count):
            keys[c, d * piece : (d + 1) * piece] = own_kv[d][:, lanes(c)]
        scores[c % 2] = dot(jnp.concatenate([keys[c], mask[...]], axis=1), q_x[c], NT)

    def second(c):
        block = scores[c % 2] * (SCALE * LOG2E)
        raised = jnp.exp2(block - jnp.max(block, axis=0, keepdims=True))
        probs = raised * (1.0 / jnp.sum(raised, axis=0, keepdims=True))
        exact[c] = probs
        probs_p[c] = probs.astype(BF16)

    def third(c):
        grad = dot(probs_p[c, piece:], g_m[c])
        for d in range(count - 1):
            near[d, :, lanes(c)] = grad[d * piece : (d + 1) * piece]

    in_turn(first, second, third)


def prompt_grads_kernel(count, q_x, g_x, exact, near_v, near_r, *refs):
    own_kv = refs[:count]
    dscore_p, values, *near, dprob = refs[count:]
    piece = own_kv[0].shape[0]

    def first(c):
        for d in range(count):
            values[c, d * piece : (d + 1) * piece] = own_kv[d][:, lanes(KVH + c)]
        dprob[c % 2] = dot(jnp.concatenate([values[c], values[c]], axis=1), g_x[c], NT)

    def second(c):
        probs = exact[c]
        weighted = probs * dprob[c % 2]
        delta = jnp.sum(weighted, axis=0, keepdims=True)
        dscore_p[c] = (weighted - probs * delta).astype(BF16)

    def third(c):
        grad = dot(dscore_p[c, piece:], q_x[c, :, :DH])
        for d in range(count - 1):
            part = grad[d * piece : (d + 1) * piece]
            near[d][0, :, lanes(c)] = near_r[d, 0, :, lanes(c)] + part
            near[d][1, :, lanes(c)] = near_r[d, 1, :, lanes(c)] + near_v[d, :, lanes(c)]

    in_turn(first, second, third)


def first_piece_kernel(
    probs_p, dscore_p, qp_x, gp_m, raised_a, dprob_a, own_t, qr_x, gr_m, chosen, near, far
):
    piece = near.shape[1]
    slots = raised_a.shape[1] - piece
    is_own = chosen[0:1, :]
    for c in range(KVH):
        probs = raised_a[c, slots:] * own_t[c, 0:1]
        dscore = (probs * (dprob_a[c, slots:] - own_t[c, 1:2])).astype(BF16)
        grads = dot(dscore, qr_x[c, :, :DH]), dot(probs.astype(BF16), gr_m[c])
        own = dot(dscore_p[c, :piece], qp_x[c, :, :DH]), dot(probs_p[c, :piece], gp_m[c])
        for i in range(2):
            near[i, :, lanes(c)] = own[i] + grads[i] * is_own
            far[i, :, lanes(c)] = (grads[i] * (1.0 - is_own)).astype(BF16)


def finish_kernel(
    keep_p, probs_p, dscore_p, keys_p, values_p, keep_r, probs_c, dscore_c, keys_a, values_a,
    keys_b, values_b, raised_a, dprob_a, own_t, k_r, v_r, q_x, g_m, out_p, dq_p, out_r, dq_r, dk_r, dv_r,
):
    c = pl.program_id(0)
    own_factor, delta = own_t[c, 0:1], own_t[c, 1:2]
    slots = k_r.shape[0]
    probs = raised_a[c] * own_factor
    dscore = (probs * (dprob_a[c] - delta)).astype(BF16)
    probs = probs.astype(BF16)
    dv_r[...] = dot(probs[:slots], g_m[c]).astype(BF16)
    dk_r[...] = dot(dscore[:slots], q_x[c, :, :DH]).astype(BF16)

    def across(block):
        return wide(block.astype(BF16).T)

    values = jnp.concatenate([v_r[...], values_a[c], values_b[c]], axis=0)
    keys = jnp.concatenate([k_r[...], keys_a[c], keys_b[c]], axis=0)
    left = beside(values, keys)
    right = jnp.concatenate([probs, probs_c[c], dscore, dscore_c[c]], axis=0)
    both = dot(left, right, TN)
    out_r[...] = across(both[:DH] * keep_r[0:1])
    dq_r[...] = across(both[DH:])
    right = jnp.concatenate([probs_p[c], dscore_p[c]], axis=0)
    both = dot(beside(values_p[c], keys_p[c]), right, TN)
    out_p[...] = across(both[:DH] * keep_p[0:1])
    dq_p[...] = across(both[DH:])


def attend(queries, cotangent, keys, values, bias, live):
    rows, count = bias.shape
    scores = (dot(queries, keys, NT) * (SCALE * LOG2E)).reshape(PER, rows, count) + bias[None]
    top = jnp.max(scores, axis=-1, keepdims=True)
    raised = jnp.exp2(scores - top)
    total = jnp.sum(raised, axis=-1, keepdims=True)
    probs = (raised * (1.0 / total)).reshape(PER * rows, count)
    half = probs.astype(BF16)
    mixed = dot(half, values).reshape(PER, rows, DH)
    result = jnp.where(live[None], mixed, 0.0).astype(BF16).reshape(PER * rows, DH)
    delta = jnp.sum(
        cotangent.astype(F32) * result.astype(F32), axis=-1, keepdims=True
    )
    dprob = dot(cotangent, values, NT)
    dscore = (probs * (dprob - delta) * SCALE).astype(BF16)
    grad_q = dot(dscore, keys).astype(BF16)
    grad_k = dot(dscore, queries, TN)
    grad_v = dot(half, cotangent, TN)
    return result, grad_q, grad_k, grad_v


def long_kernel(count, *refs):
    prompt_len, resp_len, resp_host, q_p, g_p, q_r, g_r, k_r, v_r = refs[:9]
    own_k, own_v, pair_k, pair_v = [refs[9 + i * count : 9 + (i + 1) * count] for i in range(4)]
    out_p, dq_p, out_r, dq_r, dk_r, dv_r, far, *near = refs[9 + 4 * count :]
    group = lax.axis_index("grp")
    shard = lax.axis_index("seq")
    own_length = prompt_len[group]
    owner, resp_length = hosted(resp_len, resp_host, count)
    owner_length = prompt_len[owner]
    is_own = owner == group
    piece = own_k[0].shape[0]
    rows = q_p.shape[0]
    slots = q_r.shape[0]
    span = count * piece
    column = lax.broadcasted_iota(jnp.int32, (1, span), 1)
    place = ((column // piece) ^ shard) * piece + column % piece
    position = lax.broadcasted_iota(jnp.int32, (rows, 1), 0) + shard * rows
    live = position < own_length
    allowed = (place == position) | ((place < position) & live)
    bias = jnp.where(allowed, 0.0, BLOCKED)
    keys = jnp.concatenate([ref[...] for ref in own_k], axis=0)
    values = jnp.concatenate([ref[...] for ref in own_v], axis=0)
    queries = tall(q_p[...])
    cotangent = tall(jnp.where(live, g_p[...], 0))
    result, grad_q, own_gk, own_gv = attend(queries, cotangent, keys, values, bias, live)
    out_p[...] = wide(result)
    dq_p[...] = wide(grad_q)

    slot = lax.broadcasted_iota(jnp.int32, (slots, 1), 0)
    live = slot < resp_length
    other = lax.broadcasted_iota(jnp.int32, (1, slots), 1)
    bias = jnp.concatenate(
        [
            jnp.where(live & (place < owner_length), 0.0, BLOCKED),
            jnp.where((other == slot) | ((other < slot) & live), 0.0, BLOCKED),
        ],
        axis=1,
    )
    keys = jnp.concatenate(
        [jnp.where(is_own, a[...], b[...]) for a, b in zip(own_k, pair_k)] + [k_r[...]], axis=0
    )
    values = jnp.concatenate(
        [jnp.where(is_own, a[...], b[...]) for a, b in zip(own_v, pair_v)] + [v_r[...]], axis=0
    )
    queries = tall(q_r[...])
    cotangent = tall(jnp.where(live, g_r[...], 0))
    result, grad_q, grad_k, grad_v = attend(queries, cotangent, keys, values, bias, live)
    out_r[...] = wide(result)
    dq_r[...] = wide(grad_q)
    dk_r[...] = grad_k[span:].astype(BF16)
    dv_r[...] = grad_v[span:].astype(BF16)
    for d in range(count):
        part = slice(d * piece, (d + 1) * piece)
        near[d][0] = own_gk[part] + jnp.where(is_own, grad_k[part], 0.0)
        near[d][1] = own_gv[part] + jnp.where(is_own, grad_v[part], 0.0)
        far[d, 0] = jnp.where(is_own, 0.0, grad_k[part]).astype(BF16)
        far[d, 1] = jnp.where(is_own, 0.0, grad_v[part]).astype(BF16)


def long_prompts(prompt_len, resp_len, resp_host, q_p, g_p, q_r, g_r, k_r, v_r, own, pair):
    count, rows, slots = len(own), q_p.shape[0], q_r.shape[0]
    piece, width = rows, KVH * DH

    def block(height, lanes, offset=0):
        return pl.BlockSpec((height, lanes), lambda c: (0, c + offset))

    wide_p, wide_r = block(rows, PER * DH), block(slots, PER * DH)
    return pl.pallas_call(
        lambda *refs: long_kernel(count, *refs),
        grid=(KVH,),
        in_specs=[pl.BlockSpec(memory_space=pltpu.SMEM)] * 3
        + [wide_p, wide_p, wide_r, wide_r]
        + [block(slots, DH)] * 2
        + [block(piece, DH)] * count
        + [block(piece, DH, KVH)] * count
        + [block(piece, DH)] * count
        + [block(piece, DH, KVH)] * count,
        out_specs=[wide_p, wide_p, wide_r, wide_r]
        + [block(slots, DH)] * 2
        + [pl.BlockSpec((count, 2, piece, DH), lambda c: (0, 0, 0, c))]
        + [pl.BlockSpec((2, piece, DH), lambda c: (0, 0, c))] * count,
        out_shape=[jax.ShapeDtypeStruct((rows, HQ * DH), BF16)] * 2
        + [jax.ShapeDtypeStruct((slots, HQ * DH), BF16)] * 2
        + [jax.ShapeDtypeStruct((slots, width), BF16)] * 2
        + [jax.ShapeDtypeStruct((count, 2, piece, width), BF16)]
        + [jax.ShapeDtypeStruct((2, piece, width), F32)] * count,
        compiler_params=pltpu.CompilerParams(vmem_limit_bytes=56 * 2**20),
        name="long_prompts",
    )(prompt_len, resp_len, resp_host, q_p, g_p, q_r, g_r, k_r, v_r, *own, *own, *pair, *pair)


def sent(near, back):
    return [
        swapped((a + back[d].astype(F32)).astype(BF16), "seq", d + 1) for d, a in enumerate(near)
    ]


def summed(near, back, parts):
    total = near + back.astype(F32)
    order = ORDER if len(parts) == len(ORDER) else range(1, len(parts) + 1)
    for d in order:
        total = total + parts[d - 1].astype(F32)
    return total.astype(BF16)


def collected(out_p, dq_p, out_r, dq_r, dk_r, dv_r, total):
    return tuple(
        array[None] for array in (out_p, out_r, dq_p, dq_r, total[0], total[1], dk_r, dv_r)
    )


def shards(
    prompt_len,
    resp_len,
    resp_host,
    q_prompt,
    k_prompt,
    v_prompt,
    g_prompt,
    q_resp,
    k_resp,
    v_resp,
    g_resp,
):
    count = lax.axis_size("seq")
    rows = q_prompt.shape[1]
    slots = q_resp.shape[1]
    width = KVH * DH
    span = count * rows
    vmem, hbm = [pl.BlockSpec(memory_space=space) for space in (pltpu.VMEM, pltpu.HBM)]
    resp_len, resp_host = resp_len.T, resp_host.T

    def inside(*shape, dtype=BF16):
        return pltpu.VMEM(shape, dtype)

    def held(array):
        return pltpu.with_memory_space_constraint(array, pltpu.HBM)

    def options(megabytes):
        return pltpu.CompilerParams(vmem_limit_bytes=megabytes * 2**20)

    def cost(flops):
        return pl.CostEstimate(flops=flops, bytes_accessed=2**20, transcendentals=0)

    mine = jnp.concatenate([k_prompt[0], v_prompt[0]], axis=1)
    own = [mine] + [swapped(mine, "seq", d) for d in range(1, count)]
    if span > LONG or max(rows, slots) > DH:
        pair = [swapped(part, "grp", 1) for part in own]
        out_p, dq_p, out_r, dq_r, dk_r, dv_r, far, *near = long_prompts(
            prompt_len, resp_len, resp_host, q_prompt[0], g_prompt[0], q_resp[0], g_resp[0],
            k_resp[0], v_resp[0], own, pair,
        )
        back = swapped(far, "grp", 1)
        total = summed(near[0], back[0], sent(near[1:], back[1:]))
        return collected(out_p, dq_p, out_r, dq_r, dk_r, dv_r, total)

    made = pl.pallas_call(
        lambda *refs: prepare_kernel(count, *refs),
        in_specs=[hbm] * 7,
        out_specs=[vmem] * 12,
        out_shape=[inside(KVH, PER * rows, 2 * DH)] * 2
        + [inside(KVH, PER * rows, DH)]
        + [inside(KVH, PER * slots, 2 * DH)] * 2
        + [inside(KVH, PER * slots, DH)]
        + [inside(span, DH)] * 2
        + [
            inside(slots, DH),
            inside(8, PER * rows, dtype=F32),
            inside(8, PER * slots, dtype=F32),
            inside(8, DH, dtype=F32),
        ],
        scratch_shapes=[pltpu.VMEM((rows, HQ * DH), BF16)] * 2
        + [pltpu.VMEM((slots, HQ * DH), BF16)] * 2
        + [pltpu.SMEM(t.shape, jnp.int32) for t in (prompt_len, resp_len, resp_host)]
        + [pltpu.SemaphoreType.DMA((7,))],
        compiler_params=options(20),
        cost_estimate=cost(4 * 10**9),
        name="prepare",
    )(
        held(prompt_len), held(resp_len), held(resp_host),
        held(q_prompt[0]), held(g_prompt[0]), held(q_resp[0]), held(g_resp[0]),
    )
    qp_x, gp_x, gp_m, qr_x, gr_x, gr_m, mask_p, mask_r, mask_own, *rest = made
    keep_p, keep_r, chosen = rest

    here = 1
    pair = [swapped(part, "grp", 1) for part in own[:here]]
    keys_a, values_a, raised_a, dprob_a, stats = pl.pallas_call(
        lambda *refs: early_kernel(here, *refs),
        in_specs=[vmem] * (7 + 2 * here),
        out_specs=[vmem] * 5,
        out_shape=[inside(KVH, here * rows, DH)] * 2
        + [inside(KVH, slots + here * rows, PER * slots, dtype=F32)] * 2
        + [inside(KVH, 8, PER * slots, dtype=F32)],
        scratch_shapes=[pltpu.VMEM((2, slots + here * rows, PER * slots), F32)],
        compiler_params=options(16),
        cost_estimate=cost(3 * 10**9),
        name="early",
    )(qr_x, gr_x, mask_r, mask_own, chosen, k_resp[0], v_resp[0], *own[:here], *pair)
    own[here:] = [lax.optimization_barrier((part, stats))[0] for part in own[here:]]
    pair += [swapped(part, "grp", 1) for part in own[here:]]

    exact, probs_p, keys_p, near_v = pl.pallas_call(
        lambda *refs: prompt_probs_kernel(count, *refs),
        in_specs=[vmem] * (3 + count),
        out_specs=[vmem] * 4,
        out_shape=[
            inside(KVH, span, PER * rows, dtype=F32),
            inside(KVH, span, PER * rows),
            inside(KVH, span, DH),
            inside(count - 1, rows, width, dtype=F32),
        ],
        scratch_shapes=[pltpu.VMEM((2, span, PER * rows), F32)],
        compiler_params=options(12),
        cost_estimate=cost(2 * 10**9),
        name="prompt_probs",
    )(qp_x, gp_m, mask_p, *own)

    stats, near_v = lax.optimization_barrier((stats, near_v))
    late = count - here
    probs_c, dscore_c, keys_b, values_b, own_t, near_r, far = pl.pallas_call(
        lambda *refs: response_kernel(late, *refs),
        in_specs=[vmem] * (6 + 2 * late),
        out_specs=[vmem] * 7,
        out_shape=[inside(KVH, late * rows, PER * slots)] * 2
        + [inside(KVH, late * rows, DH)] * 2
        + [
            inside(KVH, 8, PER * slots, dtype=F32),
            inside(late, 2, rows, width, dtype=F32),
            inside(late, 2, rows, width),
        ],
        scratch_shapes=[pltpu.VMEM((2, 2 * late * rows, PER * slots), F32)],
        compiler_params=options(20),
        cost_estimate=cost(3 * 10**9),
        name="responses",
    )(
        qr_x, gr_x, gr_m, mask_r, stats, chosen, *own[here:], *pair[here:]
    )
    back = swapped(far, "grp", 1)

    dscore_p, values_p, *near = pl.pallas_call(
        lambda *refs: prompt_grads_kernel(count, *refs),
        in_specs=[vmem] * (5 + count),
        out_specs=[vmem] * (1 + count),
        out_shape=[inside(KVH, span, PER * rows), inside(KVH, span, DH)]
        + [inside(2, rows, width, dtype=F32)] * (count - 1),
        scratch_shapes=[pltpu.VMEM((2, span, PER * rows), F32)],
        compiler_params=options(12),
        cost_estimate=cost(2 * 10**9),
        name="prompt_grads",
    )(qp_x, gp_x, exact, near_v, near_r, *own)

    parts = sent(near, back)

    near, far = pl.pallas_call(
        first_piece_kernel,
        in_specs=[vmem] * 10,
        out_specs=[vmem] * 2,
        out_shape=[inside(2, rows, width, dtype=F32), inside(2, rows, width)],
        compiler_params=options(8),
        cost_estimate=cost(10**9),
        name="first_piece",
    )(probs_p, dscore_p, qp_x, gp_m, raised_a, dprob_a, own_t, qr_x, gr_m, chosen)
    back = swapped(far, "grp", 1)

    def block(height, extent):
        return pl.BlockSpec((height, extent), lambda c: (0, c))

    wide_p, wide_r, own_block = block(rows, PER * DH), block(slots, PER * DH), block(slots, DH)
    out_p, dq_p, out_r, dq_r, dk_r, dv_r = pl.pallas_call(
        finish_kernel,
        grid=(KVH,),
        in_specs=[vmem] * 15 + [own_block] * 2 + [vmem] * 2,
        out_specs=[wide_p, wide_p, wide_r, wide_r, own_block, own_block],
        out_shape=[jax.ShapeDtypeStruct((rows, HQ * DH), BF16)] * 2
        + [jax.ShapeDtypeStruct((slots, HQ * DH), BF16)] * 2
        + [jax.ShapeDtypeStruct((slots, width), BF16)] * 2,
        compiler_params=options(20),
        cost_estimate=cost(8 * 10**9),
        name="finish",
    )(
        keep_p, probs_p, dscore_p, keys_p, values_p, keep_r, probs_c, dscore_c, keys_a, values_a,
        keys_b, values_b, raised_a, dprob_a, own_t, k_resp[0], v_resp[0], qr_x, gr_m,
    )
    return collected(out_p, dq_p, out_r, dq_r, dk_r, dv_r, summed(near, back, parts))


def solution(mesh):
    split = P("grp", "seq", None)
    return jax.shard_map(
        shards,
        mesh=mesh,
        in_specs=(P(), P(), P()) + (split,) * 8,
        out_specs=(split,) * 8,
        check_vma=False,
    )
```

```python
import jax
import jax.numpy as jnp
from jax import lax
from jax.experimental import pallas as pl
from jax.experimental.pallas import tpu as pltpu
from jax.sharding import PartitionSpec as P

HQ = 32
KVH = 4
DH = 128
PER = HQ // KVH
SCALE = DH ** (-0.5)
LOG2E = 1.4426950408889634
BLOCKED = -1e30
LONG = 512
ORDER = (3, 2, 1)
BF16 = jnp.bfloat16
F32 = jnp.float32
NN = (((1,), (0,)), ((), ()))
NT = (((1,), (1,)), ((), ()))
TN = (((0,), (0,)), ((), ()))


def dot(a, b, dims=NN):
    return lax.dot_general(a, b, dims, preferred_element_type=F32)


def swapped(block, axis, distance):
    count = lax.axis_size(axis)
    return lax.ppermute(block, axis, [(i, i ^ distance) for i in range(count)])


def tall(block):
    return jnp.concatenate([block[:, lanes(h)] for h in range(PER)], axis=0)


def wide(block):
    rows = block.shape[0] // PER
    return jnp.concatenate([block[h * rows : (h + 1) * rows] for h in range(PER)], axis=1)


def lanes(c, width=DH):
    return slice(c * width, (c + 1) * width)


def hosted(resp_len, resp_host, count):
    group = lax.axis_index("grp")
    first = group // 2 * 2
    slot = group % 2 * count + lax.axis_index("seq")
    owner, length = first, jnp.int32(0)
    for offset in range(2):
        for r in range(resp_host.shape[0]):
            match = resp_host[r, first + offset] == slot
            owner = jnp.where(match, first + offset, owner)
            length = jnp.where(match, resp_len[r, first + offset], length)
    return owner, length


def beside(a, b):
    blank = jnp.zeros_like(a)
    return jnp.concatenate(
        [jnp.concatenate([a, blank], axis=1), jnp.concatenate([blank, b], axis=1)], axis=0
    )


def prepare_kernel(
    count, prompt_table, len_table, host_table, q_p, g_p, q_r, g_r,
    qp_x, gp_x, gp_m, qr_x, gr_x, gr_m, mask_p, mask_r, mask_own, keep_p, keep_r, chosen,
    buf_qp, buf_gp, buf_qr, buf_gr, prompt_len, resp_len, resp_host, sems,
):
    buffers = (buf_qr, buf_gr, buf_qp, buf_gp)
    copies = [
        pltpu.make_async_copy(src, dst, sems.at[i])
        for i, (src, dst) in enumerate(zip((q_r, g_r, q_p, g_p), buffers))
    ]
    tables = [
        pltpu.make_async_copy(src, dst, sems.at[4 + i])
        for i, (src, dst) in enumerate(
            ((prompt_table, prompt_len), (len_table, resp_len), (host_table, resp_host))
        )
    ]
    for copy in tables + copies:
        copy.start()
    for copy in tables:
        copy.wait()
    shard = lax.axis_index("seq")
    owner, resp_length = hosted(resp_len, resp_host, count)
    group = lax.axis_index("grp")
    own_length, owner_length = prompt_len[group], prompt_len[owner]
    rows, slots = buf_qp.shape[0], buf_qr.shape[0]
    span = count * rows
    key = lax.broadcasted_iota(jnp.int32, (span, DH), 0)
    place = ((key // rows) ^ shard) * rows + key % rows
    lane = lax.broadcasted_iota(jnp.int32, (span, DH), 1)
    blocked_p = (place > lane + shard * rows) & (lane < rows)
    mask_p[...] = jnp.where(blocked_p, BLOCKED, 0.0).astype(BF16)
    mask_r[...] = jnp.where(place >= owner_length, BLOCKED, 0.0).astype(BF16)
    key = lax.broadcasted_iota(jnp.int32, (slots, DH), 0)
    lane = lax.broadcasted_iota(jnp.int32, (slots, DH), 1)
    mask_own[...] = jnp.where((key > lane) & (lane < slots), BLOCKED, 0.0).astype(BF16)
    hot_r = jnp.where(key == lane, 1.0, 0.0).astype(BF16)
    key = lax.broadcasted_iota(jnp.int32, (rows, DH), 0)
    lane = lax.broadcasted_iota(jnp.int32, (rows, DH), 1)
    hot_p = jnp.where(key == lane, 1.0, 0.0).astype(BF16)
    chosen[...] = jnp.zeros(chosen.shape, F32) + jnp.where(owner == group, 1.0, 0.0)
    lane = lax.broadcasted_iota(jnp.int32, keep_p.shape, 1)
    keep_p[...] = jnp.where(lane % rows + shard * rows < own_length, 1.0, 0.0)
    lane = lax.broadcasted_iota(jnp.int32, keep_r.shape, 1)
    keep_r[...] = jnp.where(lane % slots < resp_length, 1.0, 0.0)
    live_p = lax.broadcasted_iota(jnp.int32, (rows, 1), 0) + shard * rows < own_length
    live_r = lax.broadcasted_iota(jnp.int32, (slots, 1), 0) < resp_length
    def lay(c, height, q, g, live, hot, to_q, to_g, to_m):
        for h in range(PER):
            to, at = slice(h * height, (h + 1) * height), lanes(c * PER + h)
            to_q[c, to, :DH] = q[:, at]
            to_q[c, to, DH:] = hot
            kept = jnp.where(live, g[:, at], 0)
            to_m[c, to] = kept
            scaled = kept.astype(F32) * SCALE
            high = scaled.astype(BF16)
            to_g[c, to, :DH] = high
            to_g[c, to, DH:] = (scaled - high.astype(F32)).astype(BF16)

    for copy in copies[:2]:
        copy.wait()
    for c in range(KVH):
        lay(c, slots, buf_qr, buf_gr, live_r, hot_r, qr_x, gr_x, gr_m)
    for copy in copies[2:]:
        copy.wait()
    for c in range(KVH):
        lay(c, rows, buf_qp, buf_gp, live_p, hot_p, qp_x, gp_x, gp_m)


def in_turn(*stages):
    stages[0](0)
    for c in range(KVH):
        if c + 1 < KVH:
            stages[0](c + 1)
        for stage in stages[1:]:
            stage(c)


def chosen_pieces(chosen, own, pair, c, to, skip=0):
    own_half, pair_half = chosen[0:1, :].astype(BF16), (1.0 - chosen[0:1, :]).astype(BF16)
    piece = own[0].shape[0]
    for d in range(len(own)):
        to[c, d * piece : (d + 1) * piece] = (
            own[d][:, lanes(skip + c)] * own_half + pair[d][:, lanes(skip + c)] * pair_half
        )


def halves(block):
    return jnp.concatenate([block, block], axis=1)


def early_kernel(count, q_x, g_x, mask_r, mask_own, chosen, k_r, v_r, *refs):
    own, pair = refs[:count], refs[count : 2 * count]
    keys, values, raised_a, dprob_a, stats, scores = refs[2 * count :]
    span = keys.shape[1]

    def first(c):
        chosen_pieces(chosen, own, pair, c, keys)
        chosen_pieces(chosen, own, pair, c, values, KVH)
        key = jnp.concatenate([k_r[:, lanes(c)], keys[c]], axis=0)
        mask = jnp.concatenate([mask_own[...], mask_r[:span]], axis=0)
        value = jnp.concatenate([v_r[:, lanes(c)], values[c]], axis=0)
        scores[c % 2] = dot(jnp.concatenate([key, mask], axis=1), q_x[c], NT)
        dprob_a[c] = dot(halves(value), g_x[c], NT)

    def second(c):
        block = scores[c % 2] * (SCALE * LOG2E)
        top = jnp.max(block, axis=0, keepdims=True)
        raised = jnp.exp2(block - top)
        raised_a[c] = raised
        stats[c, 0:1] = top
        stats[c, 1:2] = jnp.sum(raised, axis=0, keepdims=True)
        stats[c, 2:3] = jnp.sum(raised * dprob_a[c], axis=0, keepdims=True)

    in_turn(first, second)


def response_kernel(count, q_x, g_x, g_m, mask_r, stats, chosen, *refs):
    own, pair = refs[:count], refs[count : 2 * count]
    probs_c, dscore_c, keys, values, own_t, near, far, scores = refs[2 * count :]
    piece = own[0].shape[0]
    late = count * piece
    early = mask_r.shape[0] - late
    is_own = chosen[0:1, :]
    is_pair = 1.0 - is_own

    def first(c):
        chosen_pieces(chosen, own, pair, c, keys)
        chosen_pieces(chosen, own, pair, c, values, KVH)
        scores[c % 2, :late] = dot(jnp.concatenate([keys[c], mask_r[early:]], axis=1), q_x[c], NT)
        scores[c % 2, late:] = dot(halves(values[c]), g_x[c], NT)

    def second(c):
        block = scores[c % 2, :late] * (SCALE * LOG2E)
        early_top = stats[c, 0:1]
        top = jnp.maximum(jnp.max(block, axis=0, keepdims=True), early_top)
        raised = jnp.exp2(block - top)
        early_raised = jnp.exp2(early_top - top)
        total = jnp.sum(raised, axis=0, keepdims=True) + early_raised * stats[c, 1:2]
        inverse = 1.0 / total
        factor = early_raised * inverse
        probs = raised * inverse
        weighted = probs * scores[c % 2, late:]
        delta = jnp.sum(weighted, axis=0, keepdims=True) + factor * stats[c, 2:3]
        probs_c[c] = probs.astype(BF16)
        dscore_c[c] = (weighted - probs * delta).astype(BF16)
        own_t[c, 0:1] = factor
        own_t[c, 1:2] = delta

    def third(c):
        grad_k = dot(dscore_c[c], q_x[c, :, :DH])
        grad_v = dot(probs_c[c], g_m[c])
        for d in range(count):
            part = slice(d * piece, (d + 1) * piece)
            for i, grad in enumerate((grad_k[part], grad_v[part])):
                near[d, i, :, lanes(c)] = grad * is_own
                far[d, i, :, lanes(c)] = (grad * is_pair).astype(BF16)

    in_turn(first, second, third)


def prompt_probs_kernel(count, q_x, g_m, mask, *refs):
    own_kv = refs[:count]
    exact, probs_p, keys, near, scores = refs[count:]
    piece = own_kv[0].shape[0]

    def first(c):
        for d in range(count):
            keys[c, d * piece : (d + 1) * piece] = own_kv[d][:, lanes(c)]
        scores[c % 2] = dot(jnp.concatenate([keys[c], mask[...]], axis=1), q_x[c], NT)

    def second(c):
        block = scores[c % 2] * (SCALE * LOG2E)
        raised = jnp.exp2(block - jnp.max(block, axis=0, keepdims=True))
        probs = raised * (1.0 / jnp.sum(raised, axis=0, keepdims=True))
        exact[c] = probs
        probs_p[c] = probs.astype(BF16)

    def third(c):
        grad = dot(probs_p[c, piece:], g_m[c])
        for d in range(count - 1):
            near[d, :, lanes(c)] = grad[d * piece : (d + 1) * piece]

    in_turn(first, second, third)


def prompt_grads_kernel(count, q_x, g_x, exact, near_v, near_r, *refs):
    own_kv = refs[:count]
    dscore_p, values, *near, dprob = refs[count:]
    piece = own_kv[0].shape[0]

    def first(c):
        for d in range(count):
            values[c, d * piece : (d + 1) * piece] = own_kv[d][:, lanes(KVH + c)]
        dprob[c % 2] = dot(jnp.concatenate([values[c], values[c]], axis=1), g_x[c], NT)

    def second(c):
        probs = exact[c]
        weighted = probs * dprob[c % 2]
        delta = jnp.sum(weighted, axis=0, keepdims=True)
        dscore_p[c] = (weighted - probs * delta).astype(BF16)

    def third(c):
        grad = dot(dscore_p[c, piece:], q_x[c, :, :DH])
        for d in range(count - 1):
            part = grad[d * piece : (d + 1) * piece]
            near[d][0, :, lanes(c)] = near_r[d, 0, :, lanes(c)] + part
            near[d][1, :, lanes(c)] = near_r[d, 1, :, lanes(c)] + near_v[d, :, lanes(c)]

    in_turn(first, second, third)


def first_piece_kernel(raised_a, dprob_a, own_t, qr_x, gr_m, chosen, near, far):
    piece = near.shape[1]
    slots = raised_a.shape[1] - piece
    is_own = chosen[0:1, :]
    for c in range(KVH):
        probs = raised_a[c, slots:] * own_t[c, 0:1]
        dscore = (probs * (dprob_a[c, slots:] - own_t[c, 1:2])).astype(BF16)
        grads = dot(dscore, qr_x[c, :, :DH]), dot(probs.astype(BF16), gr_m[c])
        for i in range(2):
            near[i, :, lanes(c)] = grads[i] * is_own
            far[i, :, lanes(c)] = (grads[i] * (1.0 - is_own)).astype(BF16)


def finish_kernel(
    keep_p, probs_p, dscore_p, keys_p, values_p, keep_r, probs_c, dscore_c, keys_a, values_a,
    keys_b, values_b, raised_a, dprob_a, own_t, k_r, v_r, q_x, g_m, qp_x, gp_m,
    out_p, dq_p, out_r, dq_r, dk_r, dv_r, near,
):
    c = pl.program_id(0)
    own_factor, delta = own_t[c, 0:1], own_t[c, 1:2]
    slots = k_r.shape[0]
    probs = raised_a[c] * own_factor
    dscore = (probs * (dprob_a[c] - delta)).astype(BF16)
    probs = probs.astype(BF16)
    dv_r[...] = dot(probs[:slots], g_m[c]).astype(BF16)
    dk_r[...] = dot(dscore[:slots], q_x[c, :, :DH]).astype(BF16)

    def across(block):
        return wide(block.astype(BF16).T)

    values = jnp.concatenate([v_r[...], values_a[c], values_b[c]], axis=0)
    keys = jnp.concatenate([k_r[...], keys_a[c], keys_b[c]], axis=0)
    left = beside(values, keys)
    right = jnp.concatenate([probs, probs_c[c], dscore, dscore_c[c]], axis=0)
    both = dot(left, right, TN)
    out_r[...] = across(both[:DH] * keep_r[0:1])
    dq_r[...] = across(both[DH:])
    piece = near.shape[1]
    near[0] = dot(dscore_p[c, :piece], qp_x[c, :, :DH])
    near[1] = dot(probs_p[c, :piece], gp_m[c])
    right = jnp.concatenate([probs_p[c], dscore_p[c]], axis=0)
    both = dot(beside(values_p[c], keys_p[c]), right, TN)
    out_p[...] = across(both[:DH] * keep_p[0:1])
    dq_p[...] = across(both[DH:])


def attend(queries, cotangent, keys, values, bias, live):
    rows, count = bias.shape
    scores = (dot(queries, keys, NT) * (SCALE * LOG2E)).reshape(PER, rows, count) + bias[None]
    top = jnp.max(scores, axis=-1, keepdims=True)
    raised = jnp.exp2(scores - top)
    total = jnp.sum(raised, axis=-1, keepdims=True)
    probs = (raised * (1.0 / total)).reshape(PER * rows, count)
    half = probs.astype(BF16)
    mixed = dot(half, values).reshape(PER, rows, DH)
    result = jnp.where(live[None], mixed, 0.0).astype(BF16).reshape(PER * rows, DH)
    delta = jnp.sum(
        cotangent.astype(F32) * result.astype(F32), axis=-1, keepdims=True
    )
    dprob = dot(cotangent, values, NT)
    dscore = (probs * (dprob - delta) * SCALE).astype(BF16)
    grad_q = dot(dscore, keys).astype(BF16)
    grad_k = dot(dscore, queries, TN)
    grad_v = dot(half, cotangent, TN)
    return result, grad_q, grad_k, grad_v


def long_kernel(count, *refs):
    prompt_len, resp_len, resp_host, q_p, g_p, q_r, g_r, k_r, v_r = refs[:9]
    own_k, own_v, pair_k, pair_v = [refs[9 + i * count : 9 + (i + 1) * count] for i in range(4)]
    out_p, dq_p, out_r, dq_r, dk_r, dv_r, far, *near = refs[9 + 4 * count :]
    group = lax.axis_index("grp")
    shard = lax.axis_index("seq")
    own_length = prompt_len[group]
    owner, resp_length = hosted(resp_len, resp_host, count)
    owner_length = prompt_len[owner]
    is_own = owner == group
    piece = own_k[0].shape[0]
    rows = q_p.shape[0]
    slots = q_r.shape[0]
    span = count * piece
    column = lax.broadcasted_iota(jnp.int32, (1, span), 1)
    place = ((column // piece) ^ shard) * piece + column % piece
    position = lax.broadcasted_iota(jnp.int32, (rows, 1), 0) + shard * rows
    live = position < own_length
    allowed = (place == position) | ((place < position) & live)
    bias = jnp.where(allowed, 0.0, BLOCKED)
    keys = jnp.concatenate([ref[...] for ref in own_k], axis=0)
    values = jnp.concatenate([ref[...] for ref in own_v], axis=0)
    queries = tall(q_p[...])
    cotangent = tall(jnp.where(live, g_p[...], 0))
    result, grad_q, own_gk, own_gv = attend(queries, cotangent, keys, values, bias, live)
    out_p[...] = wide(result)
    dq_p[...] = wide(grad_q)

    slot = lax.broadcasted_iota(jnp.int32, (slots, 1), 0)
    live = slot < resp_length
    other = lax.broadcasted_iota(jnp.int32, (1, slots), 1)
    bias = jnp.concatenate(
        [
            jnp.where(live & (place < owner_length), 0.0, BLOCKED),
            jnp.where((other == slot) | ((other < slot) & live), 0.0, BLOCKED),
        ],
        axis=1,
    )
    keys = jnp.concatenate(
        [jnp.where(is_own, a[...], b[...]) for a, b in zip(own_k, pair_k)] + [k_r[...]], axis=0
    )
    values = jnp.concatenate(
        [jnp.where(is_own, a[...], b[...]) for a, b in zip(own_v, pair_v)] + [v_r[...]], axis=0
    )
    queries = tall(q_r[...])
    cotangent = tall(jnp.where(live, g_r[...], 0))
    result, grad_q, grad_k, grad_v = attend(queries, cotangent, keys, values, bias, live)
    out_r[...] = wide(result)
    dq_r[...] = wide(grad_q)
    dk_r[...] = grad_k[span:].astype(BF16)
    dv_r[...] = grad_v[span:].astype(BF16)
    for d in range(count):
        part = slice(d * piece, (d + 1) * piece)
        near[d][0] = own_gk[part] + jnp.where(is_own, grad_k[part], 0.0)
        near[d][1] = own_gv[part] + jnp.where(is_own, grad_v[part], 0.0)
        far[d, 0] = jnp.where(is_own, 0.0, grad_k[part]).astype(BF16)
        far[d, 1] = jnp.where(is_own, 0.0, grad_v[part]).astype(BF16)


def long_prompts(prompt_len, resp_len, resp_host, q_p, g_p, q_r, g_r, k_r, v_r, own, pair):
    count, rows, slots = len(own), q_p.shape[0], q_r.shape[0]
    piece, width = rows, KVH * DH

    def block(height, lanes, offset=0):
        return pl.BlockSpec((height, lanes), lambda c: (0, c + offset))

    wide_p, wide_r = block(rows, PER * DH), block(slots, PER * DH)
    return pl.pallas_call(
        lambda *refs: long_kernel(count, *refs),
        grid=(KVH,),
        in_specs=[pl.BlockSpec(memory_space=pltpu.SMEM)] * 3
        + [wide_p, wide_p, wide_r, wide_r]
        + [block(slots, DH)] * 2
        + [block(piece, DH)] * count
        + [block(piece, DH, KVH)] * count
        + [block(piece, DH)] * count
        + [block(piece, DH, KVH)] * count,
        out_specs=[wide_p, wide_p, wide_r, wide_r]
        + [block(slots, DH)] * 2
        + [pl.BlockSpec((count, 2, piece, DH), lambda c: (0, 0, 0, c))]
        + [pl.BlockSpec((2, piece, DH), lambda c: (0, 0, c))] * count,
        out_shape=[jax.ShapeDtypeStruct((rows, HQ * DH), BF16)] * 2
        + [jax.ShapeDtypeStruct((slots, HQ * DH), BF16)] * 2
        + [jax.ShapeDtypeStruct((slots, width), BF16)] * 2
        + [jax.ShapeDtypeStruct((count, 2, piece, width), BF16)]
        + [jax.ShapeDtypeStruct((2, piece, width), F32)] * count,
        compiler_params=pltpu.CompilerParams(vmem_limit_bytes=56 * 2**20),
        name="long_prompts",
    )(prompt_len, resp_len, resp_host, q_p, g_p, q_r, g_r, k_r, v_r, *own, *own, *pair, *pair)


def sent(near, back):
    return [
        swapped((a + back[d].astype(F32)).astype(BF16), "seq", d + 1) for d, a in enumerate(near)
    ]


def summed(near, back, parts):
    total = near + back.astype(F32)
    order = ORDER if len(parts) == len(ORDER) else range(1, len(parts) + 1)
    for d in order:
        total = total + parts[d - 1].astype(F32)
    return total.astype(BF16)


def collected(out_p, dq_p, out_r, dq_r, dk_r, dv_r, total):
    return tuple(
        array[None] for array in (out_p, out_r, dq_p, dq_r, total[0], total[1], dk_r, dv_r)
    )


def shards(
    prompt_len,
    resp_len,
    resp_host,
    q_prompt,
    k_prompt,
    v_prompt,
    g_prompt,
    q_resp,
    k_resp,
    v_resp,
    g_resp,
):
    count = lax.axis_size("seq")
    rows = q_prompt.shape[1]
    slots = q_resp.shape[1]
    width = KVH * DH
    span = count * rows
    vmem, hbm = [pl.BlockSpec(memory_space=space) for space in (pltpu.VMEM, pltpu.HBM)]
    resp_len, resp_host = resp_len.T, resp_host.T

    def inside(*shape, dtype=BF16):
        return pltpu.VMEM(shape, dtype)

    def held(array):
        return pltpu.with_memory_space_constraint(array, pltpu.HBM)

    def options(megabytes):
        return pltpu.CompilerParams(vmem_limit_bytes=megabytes * 2**20)

    def cost(flops):
        return pl.CostEstimate(flops=flops, bytes_accessed=2**20, transcendentals=0)

    mine = jnp.concatenate([k_prompt[0], v_prompt[0]], axis=1)
    own = [mine] + [swapped(mine, "seq", d) for d in range(1, count)]
    if span > LONG or max(rows, slots) > DH:
        pair = [swapped(part, "grp", 1) for part in own]
        out_p, dq_p, out_r, dq_r, dk_r, dv_r, far, *near = long_prompts(
            prompt_len, resp_len, resp_host, q_prompt[0], g_prompt[0], q_resp[0], g_resp[0],
            k_resp[0], v_resp[0], own, pair,
        )
        back = swapped(far, "grp", 1)
        total = summed(near[0], back[0], sent(near[1:], back[1:]))
        return collected(out_p, dq_p, out_r, dq_r, dk_r, dv_r, total)

    made = pl.pallas_call(
        lambda *refs: prepare_kernel(count, *refs),
        in_specs=[hbm] * 7,
        out_specs=[vmem] * 12,
        out_shape=[inside(KVH, PER * rows, 2 * DH)] * 2
        + [inside(KVH, PER * rows, DH)]
        + [inside(KVH, PER * slots, 2 * DH)] * 2
        + [inside(KVH, PER * slots, DH)]
        + [inside(span, DH)] * 2
        + [
            inside(slots, DH),
            inside(8, PER * rows, dtype=F32),
            inside(8, PER * slots, dtype=F32),
            inside(8, DH, dtype=F32),
        ],
        scratch_shapes=[pltpu.VMEM((rows, HQ * DH), BF16)] * 2
        + [pltpu.VMEM((slots, HQ * DH), BF16)] * 2
        + [pltpu.SMEM(t.shape, jnp.int32) for t in (prompt_len, resp_len, resp_host)]
        + [pltpu.SemaphoreType.DMA((7,))],
        compiler_params=options(20),
        cost_estimate=cost(4 * 10**9),
        name="prepare",
    )(
        held(prompt_len), held(resp_len), held(resp_host),
        held(q_prompt[0]), held(g_prompt[0]), held(q_resp[0]), held(g_resp[0]),
    )
    qp_x, gp_x, gp_m, qr_x, gr_x, gr_m, mask_p, mask_r, mask_own, *rest = made
    keep_p, keep_r, chosen = rest

    here = 1
    pair = [swapped(part, "grp", 1) for part in own[:here]]
    keys_a, values_a, raised_a, dprob_a, stats = pl.pallas_call(
        lambda *refs: early_kernel(here, *refs),
        in_specs=[vmem] * (7 + 2 * here),
        out_specs=[vmem] * 5,
        out_shape=[inside(KVH, here * rows, DH)] * 2
        + [inside(KVH, slots + here * rows, PER * slots, dtype=F32)] * 2
        + [inside(KVH, 8, PER * slots, dtype=F32)],
        scratch_shapes=[pltpu.VMEM((2, slots + here * rows, PER * slots), F32)],
        compiler_params=options(16),
        cost_estimate=cost(3 * 10**9),
        name="early",
    )(qr_x, gr_x, mask_r, mask_own, chosen, k_resp[0], v_resp[0], *own[:here], *pair)
    own[here:] = [lax.optimization_barrier((part, stats))[0] for part in own[here:]]
    pair += [swapped(part, "grp", 1) for part in own[here:]]

    exact, probs_p, keys_p, near_v = pl.pallas_call(
        lambda *refs: prompt_probs_kernel(count, *refs),
        in_specs=[vmem] * (3 + count),
        out_specs=[vmem] * 4,
        out_shape=[
            inside(KVH, span, PER * rows, dtype=F32),
            inside(KVH, span, PER * rows),
            inside(KVH, span, DH),
            inside(count - 1, rows, width, dtype=F32),
        ],
        scratch_shapes=[pltpu.VMEM((2, span, PER * rows), F32)],
        compiler_params=options(12),
        cost_estimate=cost(2 * 10**9),
        name="prompt_probs",
    )(qp_x, gp_m, mask_p, *own)

    stats, near_v = lax.optimization_barrier((stats, near_v))
    late = count - here
    probs_c, dscore_c, keys_b, values_b, own_t, near_r, far = pl.pallas_call(
        lambda *refs: response_kernel(late, *refs),
        in_specs=[vmem] * (6 + 2 * late),
        out_specs=[vmem] * 7,
        out_shape=[inside(KVH, late * rows, PER * slots)] * 2
        + [inside(KVH, late * rows, DH)] * 2
        + [
            inside(KVH, 8, PER * slots, dtype=F32),
            inside(late, 2, rows, width, dtype=F32),
            inside(late, 2, rows, width),
        ],
        scratch_shapes=[pltpu.VMEM((2, 2 * late * rows, PER * slots), F32)],
        compiler_params=options(20),
        cost_estimate=cost(3 * 10**9),
        name="responses",
    )(
        qr_x, gr_x, gr_m, mask_r, stats, chosen, *own[here:], *pair[here:]
    )
    back = swapped(far, "grp", 1)

    dscore_p, values_p, *near = pl.pallas_call(
        lambda *refs: prompt_grads_kernel(count, *refs),
        in_specs=[vmem] * (5 + count),
        out_specs=[vmem] * (1 + count),
        out_shape=[inside(KVH, span, PER * rows), inside(KVH, span, DH)]
        + [inside(2, rows, width, dtype=F32)] * (count - 1),
        scratch_shapes=[pltpu.VMEM((2, span, PER * rows), F32)],
        compiler_params=options(12),
        cost_estimate=cost(2 * 10**9),
        name="prompt_grads",
    )(qp_x, gp_x, exact, near_v, near_r, *own)

    parts = sent(near, back)

    near_r, far = pl.pallas_call(
        first_piece_kernel,
        in_specs=[vmem] * 6,
        out_specs=[vmem] * 2,
        out_shape=[inside(2, rows, width, dtype=F32), inside(2, rows, width)],
        compiler_params=options(8),
        cost_estimate=cost(10**9),
        name="first_piece",
    )(raised_a, dprob_a, own_t, qr_x, gr_m, chosen)
    back = swapped(far, "grp", 1)

    def block(height, extent):
        return pl.BlockSpec((height, extent), lambda c: (0, c))

    wide_p, wide_r, own_block = block(rows, PER * DH), block(slots, PER * DH), block(slots, DH)
    own_piece = pl.BlockSpec((2, rows, DH), lambda c: (0, 0, c))
    out_p, dq_p, out_r, dq_r, dk_r, dv_r, near = pl.pallas_call(
        finish_kernel,
        grid=(KVH,),
        in_specs=[vmem] * 15 + [own_block] * 2 + [vmem] * 4,
        out_specs=[wide_p, wide_p, wide_r, wide_r, own_block, own_block, own_piece],
        out_shape=[jax.ShapeDtypeStruct((rows, HQ * DH), BF16)] * 2
        + [jax.ShapeDtypeStruct((slots, HQ * DH), BF16)] * 2
        + [jax.ShapeDtypeStruct((slots, width), BF16)] * 2
        + [inside(2, rows, width, dtype=F32)],
        compiler_params=options(20),
        cost_estimate=cost(8 * 10**9),
        name="finish",
    )(
        keep_p, probs_p, dscore_p, keys_p, values_p, keep_r, probs_c, dscore_c, keys_a, values_a,
        keys_b, values_b, raised_a, dprob_a, own_t, k_resp[0], v_resp[0], qr_x, gr_m, qp_x, gp_m,
    )
    return collected(out_p, dq_p, out_r, dq_r, dk_r, dv_r, summed(near + near_r, back, parts))


def solution(mesh):
    split = P("grp", "seq", None)
    return jax.shard_map(
        shards,
        mesh=mesh,
        in_specs=(P(), P(), P()) + (split,) * 8,
        out_specs=(split,) * 8,
        check_vma=False,
    )
```

```python
import jax
import jax.numpy as jnp
from jax import lax
from jax.experimental import pallas as pl
from jax.experimental.pallas import tpu as pltpu
from jax.sharding import PartitionSpec as P

HQ = 32
KVH = 4
DH = 128
PER = HQ // KVH
SCALE = DH ** (-0.5)
LOG2E = 1.4426950408889634
BLOCKED = -1e30
LONG = 512
ORDER = (3, 2, 1)
BF16 = jnp.bfloat16
F32 = jnp.float32
NN = (((1,), (0,)), ((), ()))
NT = (((1,), (1,)), ((), ()))
TN = (((0,), (0,)), ((), ()))


def dot(a, b, dims=NN):
    return lax.dot_general(a, b, dims, preferred_element_type=F32)


def swapped(block, axis, distance):
    count = lax.axis_size(axis)
    return lax.ppermute(block, axis, [(i, i ^ distance) for i in range(count)])


def tall(block):
    return jnp.concatenate([block[:, lanes(h)] for h in range(PER)], axis=0)


def wide(block):
    rows = block.shape[0] // PER
    return jnp.concatenate([block[h * rows : (h + 1) * rows] for h in range(PER)], axis=1)


def lanes(c, width=DH):
    return slice(c * width, (c + 1) * width)


def hosted(resp_len, resp_host, count):
    group = lax.axis_index("grp")
    first = group // 2 * 2
    slot = group % 2 * count + lax.axis_index("seq")
    owner, length = first, jnp.int32(0)
    for offset in range(2):
        for r in range(resp_host.shape[0]):
            match = resp_host[r, first + offset] == slot
            owner = jnp.where(match, first + offset, owner)
            length = jnp.where(match, resp_len[r, first + offset], length)
    return owner, length


def beside(a, b):
    blank = jnp.zeros_like(a)
    return jnp.concatenate(
        [jnp.concatenate([a, blank], axis=1), jnp.concatenate([blank, b], axis=1)], axis=0
    )


def prepare_kernel(
    count, prompt_table, len_table, host_table, q_p, g_p, q_r, g_r,
    qp_x, gp_x, gp_m, qr_x, gr_x, gr_m, mask_p, mask_r, mask_own, keep_p, keep_r, chosen,
    buf_qp, buf_gp, buf_qr, buf_gr, prompt_len, resp_len, resp_host, sems,
):
    buffers = (buf_qr, buf_gr, buf_qp, buf_gp)
    copies = [
        pltpu.make_async_copy(src, dst, sems.at[i])
        for i, (src, dst) in enumerate(zip((q_r, g_r, q_p, g_p), buffers))
    ]
    tables = [
        pltpu.make_async_copy(src, dst, sems.at[4 + i])
        for i, (src, dst) in enumerate(
            ((prompt_table, prompt_len), (len_table, resp_len), (host_table, resp_host))
        )
    ]
    for copy in tables + copies:
        copy.start()
    for copy in tables:
        copy.wait()
    shard = lax.axis_index("seq")
    owner, resp_length = hosted(resp_len, resp_host, count)
    group = lax.axis_index("grp")
    own_length, owner_length = prompt_len[group], prompt_len[owner]
    rows, slots = buf_qp.shape[0], buf_qr.shape[0]
    span = count * rows
    key = lax.broadcasted_iota(jnp.int32, (span, DH), 0)
    place = ((key // rows) ^ shard) * rows + key % rows
    lane = lax.broadcasted_iota(jnp.int32, (span, DH), 1)
    blocked_p = (place > lane + shard * rows) & (lane < rows)
    mask_p[...] = jnp.where(blocked_p, BLOCKED, 0.0).astype(BF16)
    mask_r[...] = jnp.where(place >= owner_length, BLOCKED, 0.0).astype(BF16)
    key = lax.broadcasted_iota(jnp.int32, (slots, DH), 0)
    lane = lax.broadcasted_iota(jnp.int32, (slots, DH), 1)
    mask_own[...] = jnp.where((key > lane) & (lane < slots), BLOCKED, 0.0).astype(BF16)
    hot_r = jnp.where(key == lane, 1.0, 0.0).astype(BF16)
    key = lax.broadcasted_iota(jnp.int32, (rows, DH), 0)
    lane = lax.broadcasted_iota(jnp.int32, (rows, DH), 1)
    hot_p = jnp.where(key == lane, 1.0, 0.0).astype(BF16)
    chosen[...] = jnp.zeros(chosen.shape, F32) + jnp.where(owner == group, 1.0, 0.0)
    lane = lax.broadcasted_iota(jnp.int32, keep_p.shape, 1)
    keep_p[...] = jnp.where(lane % rows + shard * rows < own_length, 1.0, 0.0)
    lane = lax.broadcasted_iota(jnp.int32, keep_r.shape, 1)
    keep_r[...] = jnp.where(lane % slots < resp_length, 1.0, 0.0)
    live_p = lax.broadcasted_iota(jnp.int32, (rows, 1), 0) + shard * rows < own_length
    live_r = lax.broadcasted_iota(jnp.int32, (slots, 1), 0) < resp_length
    def lay(c, height, q, g, live, hot, to_q, to_g, to_m):
        for h in range(PER):
            to, at = slice(h * height, (h + 1) * height), lanes(c * PER + h)
            to_q[c, to, :DH] = q[:, at]
            to_q[c, to, DH:] = hot
            kept = jnp.where(live, g[:, at], 0)
            to_m[c, to] = kept
            scaled = kept.astype(F32) * SCALE
            high = scaled.astype(BF16)
            to_g[c, to, :DH] = high
            to_g[c, to, DH:] = (scaled - high.astype(F32)).astype(BF16)

    for copy in copies[:2]:
        copy.wait()
    for c in range(KVH):
        lay(c, slots, buf_qr, buf_gr, live_r, hot_r, qr_x, gr_x, gr_m)
    for copy in copies[2:]:
        copy.wait()
    for c in range(KVH):
        lay(c, rows, buf_qp, buf_gp, live_p, hot_p, qp_x, gp_x, gp_m)


def in_turn(*stages):
    stages[0](0)
    for c in range(KVH):
        if c + 1 < KVH:
            stages[0](c + 1)
        for stage in stages[1:]:
            stage(c)


def chosen_pieces(chosen, own, pair, c, to, skip=0):
    own_half, pair_half = chosen[0:1, :].astype(BF16), (1.0 - chosen[0:1, :]).astype(BF16)
    piece = own[0].shape[0]
    for d in range(len(own)):
        to[c, d * piece : (d + 1) * piece] = (
            own[d][:, lanes(skip + c)] * own_half + pair[d][:, lanes(skip + c)] * pair_half
        )


def halves(block):
    return jnp.concatenate([block, block], axis=1)


def early_kernel(count, q_x, g_x, mask_r, mask_own, chosen, k_r, v_r, *refs):
    own, pair = refs[:count], refs[count : 2 * count]
    keys, values, raised_a, dprob_a, stats, scores = refs[2 * count :]
    span = keys.shape[1]

    def first(c):
        chosen_pieces(chosen, own, pair, c, keys)
        chosen_pieces(chosen, own, pair, c, values, KVH)
        key = jnp.concatenate([k_r[:, lanes(c)], keys[c]], axis=0)
        mask = jnp.concatenate([mask_own[...], mask_r[:span]], axis=0)
        value = jnp.concatenate([v_r[:, lanes(c)], values[c]], axis=0)
        scores[c % 2] = dot(jnp.concatenate([key, mask], axis=1), q_x[c], NT)
        dprob_a[c] = dot(halves(value), g_x[c], NT)

    def second(c):
        block = scores[c % 2] * (SCALE * LOG2E)
        top = jnp.max(block, axis=0, keepdims=True)
        raised = jnp.exp2(block - top)
        raised_a[c] = raised
        stats[c, 0:1] = top
        stats[c, 1:2] = jnp.sum(raised, axis=0, keepdims=True)
        stats[c, 2:3] = jnp.sum(raised * dprob_a[c], axis=0, keepdims=True)

    in_turn(first, second)


def response_kernel(count, q_x, g_x, g_m, mask_r, stats, chosen, *refs):
    own, pair = refs[:count], refs[count : 2 * count]
    probs_c, dscore_c, keys, values, own_t, near, far, scores = refs[2 * count :]
    piece = own[0].shape[0]
    late = count * piece
    early = mask_r.shape[0] - late
    is_own = chosen[0:1, :]
    is_pair = 1.0 - is_own

    def first(c):
        chosen_pieces(chosen, own, pair, c, keys)
        chosen_pieces(chosen, own, pair, c, values, KVH)
        scores[c % 2, :late] = dot(jnp.concatenate([keys[c], mask_r[early:]], axis=1), q_x[c], NT)
        scores[c % 2, late:] = dot(halves(values[c]), g_x[c], NT)

    def second(c):
        block = scores[c % 2, :late] * (SCALE * LOG2E)
        early_top = stats[c, 0:1]
        top = jnp.maximum(jnp.max(block, axis=0, keepdims=True), early_top)
        raised = jnp.exp2(block - top)
        early_raised = jnp.exp2(early_top - top)
        total = jnp.sum(raised, axis=0, keepdims=True) + early_raised * stats[c, 1:2]
        inverse = 1.0 / total
        factor = early_raised * inverse
        probs = raised * inverse
        weighted = probs * scores[c % 2, late:]
        delta = jnp.sum(weighted, axis=0, keepdims=True) + factor * stats[c, 2:3]
        probs_c[c] = probs.astype(BF16)
        dscore_c[c] = (weighted - probs * delta).astype(BF16)
        own_t[c, 0:1] = factor
        own_t[c, 1:2] = delta

    def third(c):
        grad_k = dot(dscore_c[c], q_x[c, :, :DH])
        grad_v = dot(probs_c[c], g_m[c])
        for d in range(count):
            part = slice(d * piece, (d + 1) * piece)
            for i, grad in enumerate((grad_k[part], grad_v[part])):
                near[d, i, :, lanes(c)] = grad * is_own
                far[d, i, :, lanes(c)] = (grad * is_pair).astype(BF16)

    in_turn(first, second, third)


def prompt_probs_kernel(count, q_x, g_m, mask, *refs):
    own_kv = refs[:count]
    exact, probs_p, keys, near, scores = refs[count:]
    piece = own_kv[0].shape[0]

    def first(c):
        for d in range(count):
            keys[c, d * piece : (d + 1) * piece] = own_kv[d][:, lanes(c)]
        scores[c % 2] = dot(jnp.concatenate([keys[c], mask[...]], axis=1), q_x[c], NT)

    def second(c):
        block = scores[c % 2] * (SCALE * LOG2E)
        raised = jnp.exp2(block - jnp.max(block, axis=0, keepdims=True))
        probs = raised * (1.0 / jnp.sum(raised, axis=0, keepdims=True))
        exact[c] = probs
        probs_p[c] = probs.astype(BF16)

    def third(c):
        grad = dot(probs_p[c, piece:], g_m[c])
        for d in range(count - 1):
            near[d, :, lanes(c)] = grad[d * piece : (d + 1) * piece]

    in_turn(first, second, third)


def prompt_grads_kernel(count, q_x, g_x, exact, near_v, near_r, *refs):
    own_kv = refs[:count]
    dscore_p, values, *near, dprob = refs[count:]
    piece = own_kv[0].shape[0]

    def first(c):
        for d in range(count):
            values[c, d * piece : (d + 1) * piece] = own_kv[d][:, lanes(KVH + c)]
        dprob[c % 2] = dot(jnp.concatenate([values[c], values[c]], axis=1), g_x[c], NT)

    def second(c):
        probs = exact[c]
        weighted = probs * dprob[c % 2]
        delta = jnp.sum(weighted, axis=0, keepdims=True)
        dscore_p[c] = (weighted - probs * delta).astype(BF16)

    def third(c):
        grad = dot(dscore_p[c, piece:], q_x[c, :, :DH])
        for d in range(count - 1):
            part = grad[d * piece : (d + 1) * piece]
            near[d][0, :, lanes(c)] = near_r[d, 0, :, lanes(c)] + part
            near[d][1, :, lanes(c)] = near_r[d, 1, :, lanes(c)] + near_v[d, :, lanes(c)]

    in_turn(first, second, third)


def first_piece_kernel(raised_a, dprob_a, own_t, qr_x, gr_m, chosen, near, far):
    piece = near.shape[1]
    slots = raised_a.shape[1] - piece
    is_own = chosen[0:1, :]
    for c in range(KVH):
        probs = raised_a[c, slots:] * own_t[c, 0:1]
        dscore = (probs * (dprob_a[c, slots:] - own_t[c, 1:2])).astype(BF16)
        grads = dot(dscore, qr_x[c, :, :DH]), dot(probs.astype(BF16), gr_m[c])
        for i in range(2):
            near[i, :, lanes(c)] = grads[i] * is_own
            far[i, :, lanes(c)] = (grads[i] * (1.0 - is_own)).astype(BF16)


def finish_kernel(
    keep_p, probs_p, dscore_p, keys_p, values_p, keep_r, probs_c, dscore_c, keys_a, values_a,
    keys_b, values_b, raised_a, dprob_a, own_t, k_r, v_r, q_x, g_m, qp_x, gp_m,
    out_p, dq_p, out_r, dq_r, dk_r, dv_r, near,
):
    c = pl.program_id(0)
    own_factor, delta = own_t[c, 0:1], own_t[c, 1:2]
    slots = k_r.shape[0]
    probs = raised_a[c] * own_factor
    dscore = (probs * (dprob_a[c] - delta)).astype(BF16)
    probs = probs.astype(BF16)
    dv_r[...] = dot(probs[:slots], g_m[c]).astype(BF16)
    dk_r[...] = dot(dscore[:slots], q_x[c, :, :DH]).astype(BF16)

    def across(block):
        return wide(block.astype(BF16).T)

    values = jnp.concatenate([v_r[...], values_a[c], values_b[c]], axis=0)
    keys = jnp.concatenate([k_r[...], keys_a[c], keys_b[c]], axis=0)
    left = beside(values, keys)
    right = jnp.concatenate([probs, probs_c[c], dscore, dscore_c[c]], axis=0)
    both = dot(left, right, TN)
    out_r[...] = across(both[:DH] * keep_r[0:1])
    dq_r[...] = across(both[DH:])
    piece = near.shape[1]
    near[0] = dot(dscore_p[c, :piece], qp_x[c, :, :DH])
    near[1] = dot(probs_p[c, :piece], gp_m[c])
    right = jnp.concatenate([probs_p[c], dscore_p[c]], axis=0)
    both = dot(beside(values_p[c], keys_p[c]), right, TN)
    out_p[...] = across(both[:DH] * keep_p[0:1])
    dq_p[...] = across(both[DH:])


def attend(queries, cotangent, keys, values, bias, live):
    rows, count = bias.shape
    scores = (dot(queries, keys, NT) * (SCALE * LOG2E)).reshape(PER, rows, count) + bias[None]
    top = jnp.max(scores, axis=-1, keepdims=True)
    raised = jnp.exp2(scores - top)
    total = jnp.sum(raised, axis=-1, keepdims=True)
    probs = (raised * (1.0 / total)).reshape(PER * rows, count)
    half = probs.astype(BF16)
    mixed = dot(half, values).reshape(PER, rows, DH)
    result = jnp.where(live[None], mixed, 0.0).astype(BF16).reshape(PER * rows, DH)
    delta = jnp.sum(
        cotangent.astype(F32) * result.astype(F32), axis=-1, keepdims=True
    )
    dprob = dot(cotangent, values, NT)
    dscore = (probs * (dprob - delta) * SCALE).astype(BF16)
    grad_q = dot(dscore, keys).astype(BF16)
    grad_k = dot(dscore, queries, TN)
    grad_v = dot(half, cotangent, TN)
    return result, grad_q, grad_k, grad_v


def long_kernel(count, *refs):
    prompt_len, resp_len, resp_host, q_p, g_p, q_r, g_r, k_r, v_r = refs[:9]
    own_k, own_v, pair_k, pair_v = [refs[9 + i * count : 9 + (i + 1) * count] for i in range(4)]
    out_p, dq_p, out_r, dq_r, dk_r, dv_r, far, *near = refs[9 + 4 * count :]
    group = lax.axis_index("grp")
    shard = lax.axis_index("seq")
    own_length = prompt_len[group]
    owner, resp_length = hosted(resp_len, resp_host, count)
    owner_length = prompt_len[owner]
    is_own = owner == group
    piece = own_k[0].shape[0]
    rows = q_p.shape[0]
    slots = q_r.shape[0]
    span = count * piece
    column = lax.broadcasted_iota(jnp.int32, (1, span), 1)
    place = ((column // piece) ^ shard) * piece + column % piece
    position = lax.broadcasted_iota(jnp.int32, (rows, 1), 0) + shard * rows
    live = position < own_length
    allowed = (place == position) | ((place < position) & live)
    bias = jnp.where(allowed, 0.0, BLOCKED)
    keys = jnp.concatenate([ref[...] for ref in own_k], axis=0)
    values = jnp.concatenate([ref[...] for ref in own_v], axis=0)
    queries = tall(q_p[...])
    cotangent = tall(jnp.where(live, g_p[...], 0))
    result, grad_q, own_gk, own_gv = attend(queries, cotangent, keys, values, bias, live)
    out_p[...] = wide(result)
    dq_p[...] = wide(grad_q)

    slot = lax.broadcasted_iota(jnp.int32, (slots, 1), 0)
    live = slot < resp_length
    other = lax.broadcasted_iota(jnp.int32, (1, slots), 1)
    bias = jnp.concatenate(
        [
            jnp.where(live & (place < owner_length), 0.0, BLOCKED),
            jnp.where((other == slot) | ((other < slot) & live), 0.0, BLOCKED),
        ],
        axis=1,
    )
    keys = jnp.concatenate(
        [jnp.where(is_own, a[...], b[...]) for a, b in zip(own_k, pair_k)] + [k_r[...]], axis=0
    )
    values = jnp.concatenate(
        [jnp.where(is_own, a[...], b[...]) for a, b in zip(own_v, pair_v)] + [v_r[...]], axis=0
    )
    queries = tall(q_r[...])
    cotangent = tall(jnp.where(live, g_r[...], 0))
    result, grad_q, grad_k, grad_v = attend(queries, cotangent, keys, values, bias, live)
    out_r[...] = wide(result)
    dq_r[...] = wide(grad_q)
    dk_r[...] = grad_k[span:].astype(BF16)
    dv_r[...] = grad_v[span:].astype(BF16)
    for d in range(count):
        part = slice(d * piece, (d + 1) * piece)
        near[d][0] = own_gk[part] + jnp.where(is_own, grad_k[part], 0.0)
        near[d][1] = own_gv[part] + jnp.where(is_own, grad_v[part], 0.0)
        far[d, 0] = jnp.where(is_own, 0.0, grad_k[part]).astype(BF16)
        far[d, 1] = jnp.where(is_own, 0.0, grad_v[part]).astype(BF16)


def long_prompts(prompt_len, resp_len, resp_host, q_p, g_p, q_r, g_r, k_r, v_r, own, pair):
    count, rows, slots = len(own), q_p.shape[0], q_r.shape[0]
    piece, width = rows, KVH * DH

    def block(height, lanes, offset=0):
        return pl.BlockSpec((height, lanes), lambda c: (0, c + offset))

    wide_p, wide_r = block(rows, PER * DH), block(slots, PER * DH)
    return pl.pallas_call(
        lambda *refs: long_kernel(count, *refs),
        grid=(KVH,),
        in_specs=[pl.BlockSpec(memory_space=pltpu.SMEM)] * 3
        + [wide_p, wide_p, wide_r, wide_r]
        + [block(slots, DH)] * 2
        + [block(piece, DH)] * count
        + [block(piece, DH, KVH)] * count
        + [block(piece, DH)] * count
        + [block(piece, DH, KVH)] * count,
        out_specs=[wide_p, wide_p, wide_r, wide_r]
        + [block(slots, DH)] * 2
        + [pl.BlockSpec((count, 2, piece, DH), lambda c: (0, 0, 0, c))]
        + [pl.BlockSpec((2, piece, DH), lambda c: (0, 0, c))] * count,
        out_shape=[jax.ShapeDtypeStruct((rows, HQ * DH), BF16)] * 2
        + [jax.ShapeDtypeStruct((slots, HQ * DH), BF16)] * 2
        + [jax.ShapeDtypeStruct((slots, width), BF16)] * 2
        + [jax.ShapeDtypeStruct((count, 2, piece, width), BF16)]
        + [jax.ShapeDtypeStruct((2, piece, width), F32)] * count,
        compiler_params=pltpu.CompilerParams(vmem_limit_bytes=56 * 2**20),
        name="long_prompts",
    )(prompt_len, resp_len, resp_host, q_p, g_p, q_r, g_r, k_r, v_r, *own, *own, *pair, *pair)


def sent(near, back):
    return [
        swapped((a + back[d].astype(F32)).astype(BF16), "seq", d + 1) for d, a in enumerate(near)
    ]


def summed(near, back, parts):
    order = ORDER if len(parts) == len(ORDER) else range(1, len(parts) + 1)
    totals = []
    for i in range(2):
        total = near[i] + back[i].astype(F32)
        for d in order:
            total = total + parts[d - 1][i].astype(F32)
        totals.append(total.astype(BF16))
    return totals


def collected(out_p, dq_p, out_r, dq_r, dk_r, dv_r, total):
    return tuple(
        array[None] for array in (out_p, out_r, dq_p, dq_r, total[0], total[1], dk_r, dv_r)
    )


def shards(
    prompt_len,
    resp_len,
    resp_host,
    q_prompt,
    k_prompt,
    v_prompt,
    g_prompt,
    q_resp,
    k_resp,
    v_resp,
    g_resp,
):
    count = lax.axis_size("seq")
    rows = q_prompt.shape[1]
    slots = q_resp.shape[1]
    width = KVH * DH
    span = count * rows
    vmem, hbm = [pl.BlockSpec(memory_space=space) for space in (pltpu.VMEM, pltpu.HBM)]
    resp_len, resp_host = resp_len.T, resp_host.T

    def inside(*shape, dtype=BF16):
        return pltpu.VMEM(shape, dtype)

    def held(array):
        return pltpu.with_memory_space_constraint(array, pltpu.HBM)

    def options(megabytes):
        return pltpu.CompilerParams(vmem_limit_bytes=megabytes * 2**20)

    def cost(flops):
        return pl.CostEstimate(flops=flops, bytes_accessed=2**20, transcendentals=0)

    mine = jnp.concatenate([k_prompt[0], v_prompt[0]], axis=1)
    own = [mine] + [swapped(mine, "seq", d) for d in range(1, count)]
    if span > LONG or max(rows, slots) > DH:
        pair = [swapped(part, "grp", 1) for part in own]
        out_p, dq_p, out_r, dq_r, dk_r, dv_r, far, *near = long_prompts(
            prompt_len, resp_len, resp_host, q_prompt[0], g_prompt[0], q_resp[0], g_resp[0],
            k_resp[0], v_resp[0], own, pair,
        )
        back = swapped(far, "grp", 1)
        total = summed(near[0], back[0], sent(near[1:], back[1:]))
        return collected(out_p, dq_p, out_r, dq_r, dk_r, dv_r, total)

    made = pl.pallas_call(
        lambda *refs: prepare_kernel(count, *refs),
        in_specs=[hbm] * 7,
        out_specs=[vmem] * 12,
        out_shape=[inside(KVH, PER * rows, 2 * DH)] * 2
        + [inside(KVH, PER * rows, DH)]
        + [inside(KVH, PER * slots, 2 * DH)] * 2
        + [inside(KVH, PER * slots, DH)]
        + [inside(span, DH)] * 2
        + [
            inside(slots, DH),
            inside(8, PER * rows, dtype=F32),
            inside(8, PER * slots, dtype=F32),
            inside(8, DH, dtype=F32),
        ],
        scratch_shapes=[pltpu.VMEM((rows, HQ * DH), BF16)] * 2
        + [pltpu.VMEM((slots, HQ * DH), BF16)] * 2
        + [pltpu.SMEM(t.shape, jnp.int32) for t in (prompt_len, resp_len, resp_host)]
        + [pltpu.SemaphoreType.DMA((7,))],
        compiler_params=options(20),
        cost_estimate=cost(4 * 10**9),
        name="prepare",
    )(
        held(prompt_len), held(resp_len), held(resp_host),
        held(q_prompt[0]), held(g_prompt[0]), held(q_resp[0]), held(g_resp[0]),
    )
    qp_x, gp_x, gp_m, qr_x, gr_x, gr_m, mask_p, mask_r, mask_own, *rest = made
    keep_p, keep_r, chosen = rest

    here = 1
    pair = [swapped(part, "grp", 1) for part in own[:here]]
    keys_a, values_a, raised_a, dprob_a, stats = pl.pallas_call(
        lambda *refs: early_kernel(here, *refs),
        in_specs=[vmem] * (7 + 2 * here),
        out_specs=[vmem] * 5,
        out_shape=[inside(KVH, here * rows, DH)] * 2
        + [inside(KVH, slots + here * rows, PER * slots, dtype=F32)] * 2
        + [inside(KVH, 8, PER * slots, dtype=F32)],
        scratch_shapes=[pltpu.VMEM((2, slots + here * rows, PER * slots), F32)],
        compiler_params=options(16),
        cost_estimate=cost(3 * 10**9),
        name="early",
    )(qr_x, gr_x, mask_r, mask_own, chosen, k_resp[0], v_resp[0], *own[:here], *pair)
    own[here:] = [lax.optimization_barrier((part, stats))[0] for part in own[here:]]
    pair += [swapped(part, "grp", 1) for part in own[here:]]

    exact, probs_p, keys_p, near_v = pl.pallas_call(
        lambda *refs: prompt_probs_kernel(count, *refs),
        in_specs=[vmem] * (3 + count),
        out_specs=[vmem] * 4,
        out_shape=[
            inside(KVH, span, PER * rows, dtype=F32),
            inside(KVH, span, PER * rows),
            inside(KVH, span, DH),
            inside(count - 1, rows, width, dtype=F32),
        ],
        scratch_shapes=[pltpu.VMEM((2, span, PER * rows), F32)],
        compiler_params=options(12),
        cost_estimate=cost(2 * 10**9),
        name="prompt_probs",
    )(qp_x, gp_m, mask_p, *own)

    stats, near_v = lax.optimization_barrier((stats, near_v))
    late = count - here
    probs_c, dscore_c, keys_b, values_b, own_t, near_r, far = pl.pallas_call(
        lambda *refs: response_kernel(late, *refs),
        in_specs=[vmem] * (6 + 2 * late),
        out_specs=[vmem] * 7,
        out_shape=[inside(KVH, late * rows, PER * slots)] * 2
        + [inside(KVH, late * rows, DH)] * 2
        + [
            inside(KVH, 8, PER * slots, dtype=F32),
            inside(late, 2, rows, width, dtype=F32),
            inside(late, 2, rows, width),
        ],
        scratch_shapes=[pltpu.VMEM((2, 2 * late * rows, PER * slots), F32)],
        compiler_params=options(20),
        cost_estimate=cost(3 * 10**9),
        name="responses",
    )(
        qr_x, gr_x, gr_m, mask_r, stats, chosen, *own[here:], *pair[here:]
    )
    back = swapped(far, "grp", 1)

    dscore_p, values_p, *near = pl.pallas_call(
        lambda *refs: prompt_grads_kernel(count, *refs),
        in_specs=[vmem] * (5 + count),
        out_specs=[vmem] * (1 + count),
        out_shape=[inside(KVH, span, PER * rows), inside(KVH, span, DH)]
        + [inside(2, rows, width, dtype=F32)] * (count - 1),
        scratch_shapes=[pltpu.VMEM((2, span, PER * rows), F32)],
        compiler_params=options(12),
        cost_estimate=cost(2 * 10**9),
        name="prompt_grads",
    )(qp_x, gp_x, exact, near_v, near_r, *own)

    parts = sent(near, back)

    near_r, far = pl.pallas_call(
        first_piece_kernel,
        in_specs=[vmem] * 6,
        out_specs=[vmem] * 2,
        out_shape=[inside(2, rows, width, dtype=F32), inside(2, rows, width)],
        compiler_params=options(8),
        cost_estimate=cost(10**9),
        name="first_piece",
    )(raised_a, dprob_a, own_t, qr_x, gr_m, chosen)
    back = swapped(far, "grp", 1)

    def block(height, extent):
        return pl.BlockSpec((height, extent), lambda c: (0, c))

    wide_p, wide_r, own_block = block(rows, PER * DH), block(slots, PER * DH), block(slots, DH)
    own_piece = pl.BlockSpec((2, rows, DH), lambda c: (0, 0, c))
    out_p, dq_p, out_r, dq_r, dk_r, dv_r, near = pl.pallas_call(
        finish_kernel,
        grid=(KVH,),
        in_specs=[vmem] * 15 + [own_block] * 2 + [vmem] * 4,
        out_specs=[wide_p, wide_p, wide_r, wide_r, own_block, own_block, own_piece],
        out_shape=[jax.ShapeDtypeStruct((rows, HQ * DH), BF16)] * 2
        + [jax.ShapeDtypeStruct((slots, HQ * DH), BF16)] * 2
        + [jax.ShapeDtypeStruct((slots, width), BF16)] * 2
        + [inside(2, rows, width, dtype=F32)],
        compiler_params=options(20),
        cost_estimate=cost(8 * 10**9),
        name="finish",
    )(
        keep_p, probs_p, dscore_p, keys_p, values_p, keep_r, probs_c, dscore_c, keys_a, values_a,
        keys_b, values_b, raised_a, dprob_a, own_t, k_resp[0], v_resp[0], qr_x, gr_m, qp_x, gp_m,
    )
    return collected(out_p, dq_p, out_r, dq_r, dk_r, dv_r, summed(near + near_r, back, parts))


def solution(mesh):
    split = P("grp", "seq", None)
    return jax.shard_map(
        shards,
        mesh=mesh,
        in_specs=(P(), P(), P()) + (split,) * 8,
        out_specs=(split,) * 8,
        check_vma=False,
    )
```
